128 devices in a mesh: state: 32 (over z, x, core), blk: 4 (over y).
Axes of the slice: x: 4, y: 4, z: 4, core: 2. Of those that a mesh axis runs over, the one named last changes fastest.
Arguments:
- snapshots: bfloat16 [32, 64, 524288], P('blk', None, 'state'), may hold values from -8 to 8
- weights: float32 [524288], P('state'), may hold values from 0.03 to 1.75
- degrees: int32 [524288], P('state'), may hold values from 0 to 383, as said below
- pivots: int32 [16, 8], P('blk'), may hold values from 0 to 524287
Outputs:
- modes: bfloat16 [16, 2, 8, 524288], P('blk', None, None, 'state')
- energy: float32 [16, 8, 384], P('blk')
The draws below stay inside these ranges and needn't reach their ends.
Inputs may be any that keep to these rules, and one draw needn't show every extreme that they name: `degrees`: the degree of row r is floor(r * 384 / 524288) or one more.
All inputs are finite; a program needn't handle non-finite values.
Results may differ from the reference program's by a relative error of at most 0.0082.
Values may be sent and summed in bfloat16 or wider, within the bound.
No kernel may reach another device: no remote copies, remote signals or barrier semaphores. Data moves between devices by JAX's collectives and lax.ppermute only.
A program may use at most 192 MiB of HBM per device.

```python
import math
import jax
import jax.numpy as jnp
from jax import lax

NB = 32
NFFT = 64
NF = 16
K = 8
DEGREES = 384
ITERS = 6
ROWS = 524288


def draw_snapshots(key, part):
    key = jax.random.fold_in(key, 11)
    subkeys = jax.random.split(key, 4)
    gain_common = jax.random.uniform(subkeys[0], (NB, 1, 1), jnp.float32, 0.3, 1.2)
    gain_own = jax.random.uniform(subkeys[1], (NB, 1, 1), jnp.float32, 0.4, 1.2)
    common = jax.random.truncated_normal(subkeys[2], -3.0, 3.0, (1, NFFT, ROWS), jnp.float32)
    own = jax.random.truncated_normal(subkeys[3], -3.0, 3.0, (NB, NFFT, ROWS), jnp.float32)
    return (gain_common * common + gain_own * own).astype(jnp.bfloat16)


def draw_weights(key, part):
    key = jax.random.fold_in(key, 12)
    position = jnp.arange(ROWS, dtype=jnp.float32) / ROWS
    radius = 0.35 + 0.65 * position
    rough = jax.random.uniform(key, (ROWS,), jnp.float32, 0.5, 1.5)
    return radius * radius * rough


def draw_degrees(key, part):
    key = jax.random.fold_in(key, 13)
    row_index = jnp.arange(ROWS, dtype=jnp.int32)
    offset = jax.random.randint(key, (ROWS,), 0, ROWS, dtype=jnp.int32)
    level = (row_index * DEGREES + offset) // ROWS
    return jnp.minimum(level, DEGREES - 1).astype(jnp.int32)


def place_ends(entries, rng, low, top_value):
    index_at = [jax.random.randint(jax.random.fold_in(rng, axis), (), 0, length) for axis, length in enumerate(entries.shape)]
    longest = entries.shape.index(max(entries.shape))
    beside = index_at[:longest] + [(index_at[longest] + 1) % entries.shape[longest]] + index_at[longest + 1:]
    return entries.at[tuple(index_at)].set(low).at[tuple(beside)].set(top_value)


def setup_inputs(seed: int = 0) -> dict:
    seeds = jax.random.split(jax.random.key(seed), 5)
    snapshots = draw_snapshots(jax.random.fold_in(seeds[4], 71), 0)
    weights = draw_weights(jax.random.fold_in(seeds[4], 71), 0)
    degrees = draw_degrees(jax.random.fold_in(seeds[4], 71), 0)
    pivots = place_ends(jax.random.randint(seeds[3], (NF, K), 0, ROWS), jax.random.fold_in(seeds[3], 1), 0, ROWS - 1).astype(jnp.int32)
    return dict(snapshots=snapshots, weights=weights, degrees=degrees, pivots=pivots)


def dft_rows(harmonics, window_len):
    steps_t = jnp.arange(window_len, dtype=jnp.int32)
    orders = jnp.arange(1, harmonics + 1, dtype=jnp.int32)
    window = 0.5 - 0.5 * jnp.cos(2.0 * math.pi * steps_t.astype(jnp.float32) / window_len)
    window_norm = jnp.sqrt(jnp.sum(window * window))
    turns = orders[:, None] * steps_t[None, :] % window_len
    argument = 2.0 * math.pi * turns.astype(jnp.float32) / window_len
    cosine = window * jnp.cos(argument) / window_norm
    sine = -window * jnp.sin(argument) / window_norm
    return jnp.stack([cosine, sine], axis=1).astype(jnp.bfloat16)

def matmul_high(left, right):
    return jnp.einsum('fab,fbk->fak', left, right, precision=lax.Precision.HIGHEST)

def orthonormal(column_re_all, column_im_all):
    count = column_re_all.shape[2]
    done_re = []
    done_im = []
    for column in range(count):
        vec_re = column_re_all[:, :, column]
        vec_im = column_im_all[:, :, column]
        for earlier in range(column):
            base_re = done_re[earlier]
            base_im = done_im[earlier]
            coef_re = lax.optimization_barrier(jnp.sum(base_re * vec_re + base_im * vec_im, axis=1, keepdims=True))
            coef_im = lax.optimization_barrier(jnp.sum(base_re * vec_im - base_im * vec_re, axis=1, keepdims=True))
            vec_re, vec_im = (vec_re - (coef_re * base_re - coef_im * base_im), vec_im - (coef_re * base_im + coef_im * base_re))
        inverse_norm = lax.rsqrt(lax.optimization_barrier(jnp.sum(vec_re * vec_re + vec_im * vec_im, axis=1, keepdims=True)) + 1e-06)
        done_re.append(vec_re * inverse_norm)
        done_im.append(vec_im * inverse_norm)
    return (jnp.stack(done_re, axis=2), jnp.stack(done_im, axis=2))

def leading_basis(gram, row_count, modes_kept):
    blocks = gram.shape[1] // 2
    herm_re = (gram[:, :blocks, :blocks] + gram[:, blocks:, blocks:]) / row_count
    herm_im = (gram[:, :blocks, blocks:] - gram[:, blocks:, :blocks]) / row_count
    block_pos = jnp.arange(blocks, dtype=jnp.float32)
    mode_pos = jnp.arange(modes_kept, dtype=jnp.float32)
    start_re = jnp.cos(math.pi * (mode_pos[None, :] + 0.5) * (block_pos[:, None] + 0.5) / blocks) * math.sqrt(2.0 / blocks)
    basis_re = jnp.broadcast_to(start_re, (gram.shape[0], blocks, modes_kept)).astype(jnp.float32)
    basis_im = jnp.zeros_like(basis_re)
    for sweep_index in range(ITERS):
        next_re = matmul_high(herm_re, basis_re) - matmul_high(herm_im, basis_im)
        next_im = matmul_high(herm_re, basis_im) + matmul_high(herm_im, basis_re)
        basis_re, basis_im = orthonormal(next_re, next_im)
    return (basis_re, basis_im)

def expansion(basis_re, basis_im):
    trans_re = jnp.swapaxes(basis_re, 1, 2)
    trans_im = jnp.swapaxes(basis_im, 1, 2)
    upper_rows = jnp.concatenate([trans_re, -trans_im], axis=2)
    lower_rows = jnp.concatenate([trans_im, trans_re], axis=2)
    return jnp.concatenate([upper_rows, lower_rows], axis=1).astype(jnp.bfloat16)

def phased(expanded, pivot_re, pivot_im, modes_kept):
    part_re = expanded[:, :modes_kept]
    part_im = expanded[:, modes_kept:]
    inverse_mag = lax.rsqrt(pivot_re * pivot_re + pivot_im * pivot_im + 1.0)[:, :, None]
    scale_re = pivot_re[:, :, None]
    scale_im = pivot_im[:, :, None]
    out_re = (part_re * scale_re + part_im * scale_im) * inverse_mag
    out_im = (part_im * scale_re - part_re * scale_im) * inverse_mag
    return (out_re, out_im)

def reference(snapshots, weights, degrees, pivots):
    dft_table = dft_rows(NF, NFFT)

    def per_freq(inputs):
        rows_table, pivot_rows = inputs
        spectra = jnp.einsum('ct,btr->cbr', rows_table.astype(jnp.float32), snapshots.astype(jnp.float32)).astype(jnp.bfloat16)
        stacked = spectra.reshape(2 * NB, ROWS)
        weighted = (stacked * weights).astype(jnp.bfloat16)
        gram = jnp.dot(stacked, weighted.T, preferred_element_type=jnp.float32)[None]
        basis_re, basis_im = leading_basis(gram, ROWS, K)
        expand_mat = expansion(basis_re, basis_im)
        expanded = jnp.dot(expand_mat[0], stacked, preferred_element_type=jnp.float32)[None]
        pivot_re = jnp.take_along_axis(expanded[0, :K], pivot_rows[:, None], axis=1)[:, 0][None]
        pivot_im = jnp.take_along_axis(expanded[0, K:], pivot_rows[:, None], axis=1)[:, 0][None]
        out_re, out_im = phased(expanded, pivot_re, pivot_im, K)
        weighted_sq = weights * (out_re[0] * out_re[0] + out_im[0] * out_im[0])
        energy = jax.ops.segment_sum(weighted_sq.T, degrees, num_segments=DEGREES).T * (DEGREES / ROWS)
        modes_out = jnp.stack([out_re[0], out_im[0]], axis=0).astype(jnp.bfloat16)
        return (modes_out, energy)
    modes, energy = lax.map(per_freq, (dft_table, pivots))
    return (modes, energy)
```

```python
import math

import jax
import jax.numpy as jnp
import numpy as np
from jax import lax
from jax.experimental import pallas as pl
from jax.experimental.pallas import tpu as pltpu
from jax.sharding import Mesh
from jax.sharding import PartitionSpec as P

NF = 16
DEGREES = 384
ITERS = 6
MODES = 8
WINDOW = 64
GROUPS = 4
PER_GROUP = 8
OWNED = 4
PAIR = 2
HALVES = 2
BLOCKS = GROUPS * PER_GROUP
STATE = (4, 4, 2)
DEVICES = 32
LEVELS = DEGREES // DEVICES
F32 = jnp.float32
BF16 = jnp.bfloat16
VMEM = 48 * 1024 * 1024


def dft_table():
    t = np.arange(WINDOW, dtype=np.int32)
    order = np.arange(1, NF + 1, dtype=np.int32)
    two_pi = np.float32(2.0 * math.pi)
    window = np.float32(0.5) - np.float32(0.5) * np.cos(two_pi * t.astype(np.float32) / np.float32(WINDOW))
    norm = np.sqrt(np.sum(window * window))
    turns = order[:, None] * t[None, :] % WINDOW
    angle = two_pi * turns.astype(np.float32) / np.float32(WINDOW)
    table = np.stack([window * np.cos(angle) / norm, -window * np.sin(angle) / norm], axis=1)
    return table.astype(BF16)


def spectral_lhs():
    table = dft_table()
    lhs = np.zeros((GROUPS, OWNED, 2, PER_GROUP, PER_GROUP, WINDOW), dtype=BF16)
    for owner in range(GROUPS):
        for i in range(OWNED):
            for b in range(PER_GROUP):
                lhs[owner, i, :, b, b, :] = table[OWNED * owner + i]
    return lhs.reshape(GROUPS, OWNED * 2 * PER_GROUP, PER_GROUP * WINDOW)


def start_basis():
    b = np.arange(BLOCKS, dtype=np.float32)
    j = np.arange(MODES, dtype=np.float32)
    v0 = np.cos(np.float32(math.pi) * (j[:, None] + np.float32(0.5)) * (b[None, :] + np.float32(0.5)) / np.float32(BLOCKS))
    v0 = (v0 * np.float32(math.sqrt(2.0 / BLOCKS))).reshape(MODES, GROUPS, PER_GROUP)
    out = np.zeros((GROUPS, 2, MODES, 2, GROUPS, 2, PER_GROUP), dtype=np.float32)
    for y in range(GROUPS):
        for slot in range(GROUPS):
            for part in range(2):
                out[y, part, :, :, slot, part, :] = v0[:, None, (y - slot) % GROUPS]
    return out.reshape(GROUPS, 2, MODES, 128)


def spectra_call(place, snapshots, half, tile):
    blocks_dev, window_len, rows_dev = snapshots.shape
    rows = OWNED * 2 * PER_GROUP
    depth = blocks_dev * window_len
    part = rows_dev // HALVES
    steps = part // tile
    lhs_all = jnp.asarray(spectral_lhs())

    def kernel(place_ref, lhs_ref, x_ref, *rest):
        outs, lhs = rest[:-1], rest[-1]

        @pl.when(pl.program_id(0) == 0)
        def _():
            for slot in range(GROUPS):
                owner = lax.rem(place_ref[0] + slot, GROUPS)
                lhs[slot * rows : (slot + 1) * rows, :] = lhs_ref[owner]

        data = x_ref[...].reshape(depth, tile)
        result = jnp.dot(lhs[...], data, preferred_element_type=F32).astype(BF16)
        for n, out in enumerate(outs):
            out[...] = result[n * 32 : (n + 1) * 32]

    out = pl.pallas_call(
        kernel,
        grid_spec=pltpu.PrefetchScalarGridSpec(
            num_scalar_prefetch=1,
            grid=(steps,),
            in_specs=[
                pl.BlockSpec((GROUPS, rows, depth), lambda n, p: (0, 0, 0)),
                pl.BlockSpec((blocks_dev, window_len, tile), lambda n, p: (0, 0, n + half * steps)),
            ],
            out_specs=[pl.BlockSpec((32, tile), lambda n, p: (0, n))] * (GROUPS * PAIR),
            scratch_shapes=[pltpu.VMEM((GROUPS * rows, depth), BF16)],
        ),
        out_shape=[jax.ShapeDtypeStruct((32, part), BF16)] * (GROUPS * PAIR),
        compiler_params=pltpu.CompilerParams(vmem_limit_bytes=VMEM),
        cost_estimate=pl.CostEstimate(
            flops=2 * GROUPS * rows * depth * part,
            bytes_accessed=2 * (depth + GROUPS * rows) * part,
            transcendentals=0,
        ),
        name="spectra",
    )(place, lhs_all, snapshots)
    return [[out[slot * PAIR + i] for slot in range(GROUPS)] for i in range(PAIR)]


def odd_lanes(shape):
    return (lax.broadcasted_iota(jnp.int32, shape, len(shape) - 1) & 8) == 8


def low_lanes(shape):
    return lax.broadcasted_iota(jnp.int32, shape, len(shape) - 1) < 64


def turned(value):
    axis = value.ndim - 1
    return jnp.where(
        odd_lanes(value.shape), pltpu.roll(value, 8, axis), -pltpu.roll(value, 120, axis)
    )


def gram_call(half, pieces, weights, pivot_local, before, tile):
    part = pieces[0].shape[1]
    steps = part // tile

    def kernel(p_ref, w_ref, *rest):
        x_refs, rest = rest[:GROUPS], rest[GROUPS:]
        out_ref, acc = rest[-2:]
        n = pl.program_id(0)

        @pl.when(n == 0)
        def _():
            acc[...] = jnp.zeros_like(acc)

        lane = lax.broadcasted_iota(jnp.int32, (MODES, tile), 1) + (n + half * steps) * tile
        for f in range(PAIR):
            x = jnp.concatenate([r[16 * f : 16 * f + 16] for r in x_refs], axis=0)
            wx = x.astype(F32) * w_ref[...]
            hot = jnp.where(lane == p_ref[f], 1.0, 0.0)
            left = jnp.concatenate([wx, hot, jnp.zeros_like(hot)], axis=0).astype(BF16)
            acc[f, :, :64] += lax.dot_general(
                left, x, (((1,), (1,)), ((), ())), preferred_element_type=F32
            )

        @pl.when(n == steps - 1)
        def _():
            for f in range(PAIR):
                total = acc[f]
                total = total + pltpu.roll(total, 64, 1)
                g = total[:64].reshape(GROUPS, 2, PER_GROUP, 128)
                upper = g[:, 0].reshape(BLOCKS, 128)
                lower = g[:, 1].reshape(BLOCKS, 128)
                cross = jnp.where(
                    odd_lanes(upper.shape),
                    pltpu.roll(lower, 8, 1) - upper,
                    upper + pltpu.roll(lower, 120, 1),
                )
                packed = jnp.where(low_lanes((16, 128)), cross[:16], cross[16:])
                packed = jnp.concatenate([packed, total[64:72]], axis=0)
                if before is not None:
                    packed = packed + rest[0][f]
                out_ref[f] = packed

    whole = pl.BlockSpec((PAIR, 24, 128), lambda n: (0, 0, 0))
    return pl.pallas_call(
        kernel,
        grid=(steps,),
        in_specs=[
            pl.BlockSpec((PAIR, MODES, 1), lambda n: (0, 0, 0)),
            pl.BlockSpec((1, tile), lambda n: (0, n + half * steps)),
        ]
        + [pl.BlockSpec((32, tile), lambda n: (0, n))] * GROUPS
        + [whole] * (before is not None),
        out_specs=whole,
        out_shape=jax.ShapeDtypeStruct((PAIR, 24, 128), F32),
        scratch_shapes=[pltpu.VMEM((PAIR, 80, 128), F32)],
        compiler_params=pltpu.CompilerParams(vmem_limit_bytes=VMEM),
        cost_estimate=pl.CostEstimate(
            flops=2 * PAIR * 64 * 256 * part, bytes_accessed=4 * 64 * part, transcendentals=0
        ),
        name="gram",
    )(pivot_local, weights, *pieces, *([] if before is None else [before]))


def split3(value):
    high = value.astype(BF16)
    rest = value - high.astype(F32)
    mid = rest.astype(BF16)
    low = (rest - mid.astype(F32)).astype(BF16)
    return high, mid, low


def right_side(cross):
    turn = turned(cross)
    full = jnp.concatenate(
        [
            piece
            for g in range(GROUPS)
            for piece in (cross[8 * g : 8 * g + 8], turn[8 * g : 8 * g + 8])
        ],
        axis=0,
    )
    full = jnp.concatenate([full, turned(full)], axis=1)
    high, mid, low = split3(full)
    return jnp.concatenate([high, mid, high, mid, low, high], axis=0)


def leading_basis(crosses, begin):
    count = len(crosses)
    rights = [right_side(cross) for cross in crosses]
    vec = jnp.stack([begin[0]] * count)
    alt = jnp.stack([begin[1]] * count)
    low_lane = low_lanes((MODES, 128))
    row = lax.broadcasted_iota(jnp.int32, (count, MODES, 1), 1)
    for _ in range(ITERS):
        new = []
        for f in range(count):
            high, mid, low = split3(vec[f])
            mixed = jnp.where(low_lane, high.astype(F32), low.astype(F32)).astype(BF16)
            left = jnp.concatenate([high, mid, mixed], axis=1)
            new.append(jnp.dot(left, rights[f], preferred_element_type=F32))
        new = jnp.stack(new)
        vec, alt = new[:, :, :128], new[:, :, 128:]
        scale = jnp.ones((count, MODES, 1), F32)
        for j in range(MODES):
            q = jnp.broadcast_to(vec[:, j : j + 1], vec.shape)
            q_alt = jnp.broadcast_to(alt[:, j : j + 1], vec.shape)
            power = jnp.sum(q * q, axis=2, keepdims=True)
            scale = jnp.where(row == j, lax.rsqrt(power * 0.5 + 1e-06), scale)
            if j < MODES - 1:
                inverse = jnp.where(row > j, 1.0 / (power + 2e-06), 0.0)
                coef_re = jnp.sum(vec * q, axis=2, keepdims=True) * inverse
                coef_im = jnp.sum(vec * q_alt, axis=2, keepdims=True) * inverse
                vec, alt = (
                    vec - (coef_re * q + coef_im * q_alt),
                    alt - (coef_re * q_alt - coef_im * q),
                )
        vec = vec * scale
        alt = alt * scale
    return vec, alt


def modes_call(pair, place, start, weights, degrees, sums, early, late, before, row_count, tile):
    rows_dev = weights.shape[1]
    steps = rows_dev // tile
    part_steps = steps // HALVES
    bands = tile * DEGREES // row_count

    def kernel(place_ref, start_ref, w_ref, deg_ref, sum_ref, *rest):
        x_refs, rest = rest[: HALVES * GROUPS], rest[HALVES * GROUPS :]
        modes_ref, energy_ref, expand, phase = rest[-4:]
        n = pl.program_id(0)

        @pl.when(n == 0)
        def _():
            total = jnp.sum(sum_ref[...], axis=0)
            crosses = []
            for f in range(PAIR):
                packed = total[f, :16] * (1.0 / row_count)
                swap = pltpu.roll(packed, 64, 1)
                low = low_lanes(packed.shape)
                crosses.append(
                    jnp.concatenate(
                        [jnp.where(low, packed, swap), jnp.where(low, swap, packed)], axis=0
                    )
                )
            vec, alt = leading_basis(crosses, start_ref[place_ref[0]])
            odd = odd_lanes(vec.shape)
            low = low_lanes(vec.shape)
            upper = jnp.where(odd, -vec, vec).astype(BF16).astype(F32)
            lower = jnp.where(odd, alt, -alt).astype(BF16).astype(F32)
            at = jnp.where(low, total[:, 16:24], 0.0)
            z_re = jnp.sum(upper * at, axis=2, keepdims=True)
            z_im = jnp.sum(lower * at, axis=2, keepdims=True)
            inverse = lax.rsqrt(z_re * z_re + z_im * z_im + 1.0)
            phase[0] = jnp.broadcast_to(z_re * inverse, vec.shape)
            phase[1] = jnp.broadcast_to(z_im * inverse, vec.shape)
            expand[:, :8] = upper
            expand[:, 8:] = lower
            energy_ref[...] = jnp.zeros_like(energy_ref) if before is None else rest[1][...]

        w = w_ref[...]
        base = place_ref[1] + n * bands
        lane = lax.broadcasted_iota(jnp.int32, (MODES, 128), 1)
        first = n < part_steps
        for f in range(PAIR):
            rows = slice(16 * f, 16 * f + 16)
            x = jnp.concatenate(
                [
                    jnp.where(first, x_refs[k][rows], x_refs[GROUPS + k][rows])
                    for k in range(GROUPS)
                ],
                axis=0,
            )
            psi = jnp.dot(expand[f][:, :64].astype(BF16), x, preferred_element_type=F32)
            s_re = phase[0, f, :, :1]
            s_im = phase[1, f, :, :1]
            p_re, p_im = psi[:8], psi[8:]
            out_re = p_re * s_re + p_im * s_im
            out_im = p_im * s_re - p_re * s_im
            modes_ref[f, 0] = out_re.astype(BF16)
            modes_ref[f, 1] = out_im.astype(BF16)
            power = w * (out_re * out_re + out_im * out_im)
            for m in range(bands + 1):
                level = jnp.sum(
                    jnp.where(deg_ref[...] == base + m, power, 0.0), axis=1, keepdims=True
                )
                spot = (pair * PAIR + f) * 32 + place_ref[2] + n * bands + m
                energy_ref[...] += jnp.where(lane == spot, level * (DEGREES / row_count), 0.0)

    in_specs = [
        pl.BlockSpec((GROUPS, 2, MODES, 128), lambda n, p: (0, 0, 0, 0)),
        pl.BlockSpec((1, tile), lambda n, p: (0, n)),
        pl.BlockSpec((1, tile), lambda n, p: (0, n)),
        pl.BlockSpec(sums.shape, lambda n, p: (0, 0, 0, 0)),
    ]
    in_specs += [
        pl.BlockSpec((32, tile), lambda n, p: (0, jnp.minimum(n, part_steps - 1)))
    ] * GROUPS
    in_specs += [
        pl.BlockSpec((32, tile), lambda n, p: (0, jnp.maximum(n - part_steps, 0)))
    ] * GROUPS
    args = [place, start, weights, degrees, sums, *early, *late]
    aliases = {}
    if before is not None:
        in_specs += [
            pl.BlockSpec(memory_space=pl.ANY),
            pl.BlockSpec((MODES, 128), lambda n, p: (0, 0)),
        ]
        aliases = {len(args): 0}
        args += list(before)
    return pl.pallas_call(
        kernel,
        grid_spec=pltpu.PrefetchScalarGridSpec(
            num_scalar_prefetch=1,
            grid=(steps,),
            in_specs=in_specs,
            out_specs=[
                pl.BlockSpec((PAIR, 2, MODES, tile), lambda n, p: (pair, 0, 0, n)),
                pl.BlockSpec((MODES, 128), lambda n, p: (0, 0)),
            ],
            scratch_shapes=[
                pltpu.VMEM((PAIR, 16, 128), F32),
                pltpu.VMEM((2, PAIR, MODES, 128), F32),
            ],
        ),
        out_shape=[
            jax.ShapeDtypeStruct((OWNED, 2, MODES, rows_dev), BF16),
            jax.ShapeDtypeStruct((MODES, 128), F32),
        ],
        input_output_aliases=aliases,
        compiler_params=pltpu.CompilerParams(vmem_limit_bytes=VMEM),
        cost_estimate=pl.CostEstimate(
            flops=2 * PAIR * 64 * 256 * rows_dev + 10**9,
            bytes_accessed=PAIR * 2 * 80 * rows_dev,
            transcendentals=0,
        ),
        name="modes",
    )(*args)


def energy_call(gathered):
    chips = gathered.shape[0]

    def kernel(in_ref, out_ref):
        out_ref[...] = jnp.zeros_like(out_ref)
        lane = lax.broadcasted_iota(jnp.int32, (MODES, 128), 1)
        for c in range(chips):
            value = in_ref[c]
            for f in range(OWNED):
                begin = c * 2 * LEVELS
                piece = jnp.where((lane >= 32 * f) & (lane < 32 * f + 2 * LEVELS + 1), value, 0.0)
                shift = (begin - 32 * f) % 128
                piece = pltpu.roll(piece, shift, 1) if shift else piece
                column = begin // 128
                split = 128 - begin % 128
                if split >= 2 * LEVELS + 1:
                    out_ref[f, :, column * 128 : column * 128 + 128] += piece
                else:
                    head = jnp.where(lane >= begin % 128, piece, 0.0)
                    out_ref[f, :, column * 128 : column * 128 + 128] += head
                    if (column + 1) * 128 < DEGREES:
                        out_ref[f, :, (column + 1) * 128 : (column + 2) * 128] += piece - head

    return pl.pallas_call(
        kernel,
        out_shape=jax.ShapeDtypeStruct((OWNED, MODES, DEGREES), F32),
        name="energy",
    )(gathered)


def gather_chips(value):
    value = value + lax.ppermute(value, "core", [(0, 1), (1, 0)])
    chips = STATE[0] * STATE[1]
    spread = jnp.broadcast_to(value[None], (chips,) + value.shape)
    return lax.all_to_all(spread, ("z", "x"), 0, 0, tiled=True)


def per_device(snapshots, weights, degrees, pivots):
    rows_dev = snapshots.shape[2]
    row_count = rows_dev * DEVICES
    core = lax.axis_index("core").astype(jnp.int32)
    state = (lax.axis_index(("z", "x", "core"))).astype(jnp.int32)
    y = lax.axis_index("blk").astype(jnp.int32)
    place = jnp.stack([y, state * LEVELS, core * LEVELS])
    pivot_local = (pivots - state * rows_dev)[:, :, None]
    weights = weights.reshape(1, rows_dev)
    degrees = degrees.reshape(1, rows_dev)
    start = jnp.asarray(start_basis())

    halves = [spectra_call(place, snapshots, half, 2048) for half in range(HALVES)]
    pieces = {}
    for pair in range(PAIR):
        for half in range(HALVES):
            sent = halves[half][pair]
            pieces[pair, half] = [sent[0]] + [
                lax.ppermute(sent[k], "blk", [(g, (g + k) % GROUPS) for g in range(GROUPS)])
                for k in range(1, GROUPS)
            ]
    before = None
    for pair in range(PAIR):
        gram = None
        for half in range(HALVES):
            gram = gram_call(
                half, pieces[pair, half], weights, pivot_local[PAIR * pair : PAIR * pair + PAIR], gram, 4096
            )
        before = modes_call(
            pair, place, start, weights, degrees, gather_chips(gram),
            pieces[pair, 0], pieces[pair, 1], before, row_count, 4096,
        )
    modes, energy = before
    return modes, energy_call(gather_chips(energy))


def solution(mesh):
    fine = Mesh(mesh.devices.reshape(*STATE, GROUPS), ("z", "x", "core", "blk"))
    state = ("z", "x", "core")
    return jax.shard_map(
        per_device,
        mesh=fine,
        in_specs=(P("blk", None, state), P(state), P(state), P("blk", None)),
        out_specs=(P("blk", None, None, state), P("blk", None, None)),
        check_vma=False,
    )
```

```python
import functools
import math

import jax
import jax.numpy as jnp
import numpy as np
from jax import lax
from jax.experimental import pallas as pl
from jax.experimental.pallas import tpu as pltpu
from jax.sharding import Mesh
from jax.sharding import PartitionSpec as P

NF = 16
DEGREES = 384
ITERS = 6
MODES = 8
WINDOW = 64
GROUPS = 4
PER_GROUP = 8
QUAD = 4
OWNED = 4
PAIR = 2
HALVES = 2
BLOCKS = GROUPS * PER_GROUP
STATE = (4, 4, 2)
DEVICES = 32
LEVELS = DEGREES // DEVICES
F32 = jnp.float32
BF16 = jnp.bfloat16
LARGE = 60 * 1024 * 1024
SMALL = 24 * 1024 * 1024


def dft_table():
    t = np.arange(WINDOW, dtype=np.int32)
    order = np.arange(1, NF + 1, dtype=np.int32)
    two_pi = np.float32(2.0 * math.pi)
    window = np.float32(0.5) - np.float32(0.5) * np.cos(two_pi * t.astype(np.float32) / np.float32(WINDOW))
    norm = np.sqrt(np.sum(window * window))
    turns = order[:, None] * t[None, :] % WINDOW
    angle = two_pi * turns.astype(np.float32) / np.float32(WINDOW)
    table = np.stack([window * np.cos(angle) / norm, -window * np.sin(angle) / norm], axis=1)
    return table.astype(BF16)


def spectral_lhs():
    table = dft_table()
    lhs = np.zeros((GROUPS, OWNED, 2, QUAD, QUAD, WINDOW), dtype=BF16)
    for owner in range(GROUPS):
        for i in range(OWNED):
            for b in range(QUAD):
                lhs[owner, i, :, b, b, :] = table[OWNED * owner + i]
    return lhs.reshape(GROUPS, OWNED * 2 * QUAD, QUAD * WINDOW)


def start_basis():
    b = np.arange(BLOCKS, dtype=np.float32)
    j = np.arange(MODES, dtype=np.float32)
    v0 = np.cos(np.float32(math.pi) * (j[:, None] + np.float32(0.5)) * (b[None, :] + np.float32(0.5)) / np.float32(BLOCKS))
    v0 = (v0 * np.float32(math.sqrt(2.0 / BLOCKS))).reshape(MODES, GROUPS, 2, QUAD)
    out = np.zeros((GROUPS, 2, MODES, 2, GROUPS, 2, 2, QUAD), dtype=np.float32)
    for y in range(GROUPS):
        for slot in range(GROUPS):
            for part in range(2):
                out[y, part, :, :, slot, :, part, :] = v0[:, None, (y - slot) % GROUPS]
    return out.reshape(GROUPS, 2, MODES, 128)


def spectra_call(snapshots, half, tile):
    blocks_dev, window_len, rows_dev = snapshots.shape
    rows = OWNED * 2 * QUAD
    depth = QUAD * window_len
    part = rows_dev // HALVES
    steps = part // tile
    lhs_all = jnp.asarray(spectral_lhs())

    def kernel(lhs_ref, x_ref, *rest):
        outs, lhs = rest[:-1], rest[-1]

        @pl.when(pl.program_id(0) == 0)
        def _():
            for slot in range(GROUPS):
                owner = lax.rem(lax.axis_index("blk") + slot, GROUPS)
                lhs[slot * rows : (slot + 1) * rows, :] = lhs_ref[owner]

        data = x_ref[...].reshape(2, depth, tile)
        result = [jnp.dot(lhs[...], data[q], preferred_element_type=F32) for q in range(2)]
        for n, out in enumerate(outs):
            out[...] = jnp.concatenate(
                [
                    result[q][8 * m : 8 * m + 8]
                    for m in range(PAIR * n, PAIR * n + PAIR)
                    for q in range(2)
                ],
                axis=0,
            ).astype(BF16)

    out = pl.pallas_call(
        kernel,
        grid=(steps,),
        in_specs=[
            pl.BlockSpec((GROUPS, rows, depth), lambda n: (0, 0, 0)),
            pl.BlockSpec((blocks_dev, window_len, tile), lambda n: (0, 0, n + half * steps)),
        ],
        out_specs=[pl.BlockSpec((32, tile), lambda n: (0, n))] * (GROUPS * PAIR),
        scratch_shapes=[pltpu.VMEM((GROUPS * rows, depth), BF16)],
        out_shape=[jax.ShapeDtypeStruct((32, part), BF16)] * (GROUPS * PAIR),
        compiler_params=pltpu.CompilerParams(vmem_limit_bytes=LARGE),
        cost_estimate=pl.CostEstimate(
            flops=4 * GROUPS * rows * depth * part,
            bytes_accessed=4 * (depth + GROUPS * rows) * part,
            transcendentals=0,
        ),
        name="spectra",
    )(lhs_all, snapshots)
    return [[out[slot * PAIR + i] for slot in range(GROUPS)] for i in range(PAIR)]


def odd_lanes(shape):
    return (lax.broadcasted_iota(jnp.int32, shape, len(shape) - 1) & QUAD) == QUAD


def low_lanes(shape):
    return lax.broadcasted_iota(jnp.int32, shape, len(shape) - 1) < 64


def low_rows(shape):
    return lax.broadcasted_iota(jnp.int32, shape, len(shape) - 2) % 8 < QUAD


def other_lanes(value):
    axis = value.ndim - 1
    return jnp.where(
        odd_lanes(value.shape), pltpu.roll(value, QUAD, axis), pltpu.roll(value, 128 - QUAD, axis)
    )


def other_rows(value):
    rows = value.shape[0]
    return pltpu.roll(value.reshape(rows // 8, 8, 128), QUAD, 1).reshape(rows, 128)


def turned(value):
    other = other_lanes(value)
    return jnp.where(odd_lanes(value.shape), other, -other)


def gram_call(half, pieces, weights, pivot_local, before, tile):
    part = pieces[0].shape[1]
    steps = part // tile

    def kernel(p_ref, w_ref, *rest):
        x_refs, rest = rest[:GROUPS], rest[GROUPS:]
        out_ref, acc = rest[-2:]
        n = pl.program_id(0)

        @pl.when(n == 0)
        def _():
            acc[...] = jnp.zeros_like(acc)

        lane = lax.broadcasted_iota(jnp.int32, (MODES, tile), 1) + (n + half * steps) * tile
        for f in range(PAIR):
            x = jnp.concatenate([r[16 * f : 16 * f + 16] for r in x_refs], axis=0)
            wx = x.astype(F32) * w_ref[...]
            hot = jnp.where(lane == p_ref[f], 1.0, 0.0)
            left = jnp.concatenate([wx, hot, jnp.zeros_like(hot)], axis=0).astype(BF16)
            acc[f, :, :64] += lax.dot_general(
                left, x, (((1,), (1,)), ((), ())), preferred_element_type=F32
            )

        @pl.when(n == steps - 1)
        def _():
            for f in range(PAIR):
                total = acc[f]
                total = total + pltpu.roll(total, 64, 1)
                gram = total[:64]
                same = low_rows(gram.shape) != odd_lanes(gram.shape)
                cross = other_lanes(other_rows(gram)) + jnp.where(same, gram, -gram)
                cross = jnp.where(low_rows((32, 128)), cross[:32], other_rows(cross[32:]))
                packed = jnp.where(low_lanes((16, 128)), cross[:16], cross[16:])
                packed = jnp.concatenate([packed, total[64:72]], axis=0)
                if before is not None:
                    packed = packed + rest[0][f]
                out_ref[f] = packed

    whole = pl.BlockSpec((PAIR, 24, 128), lambda n: (0, 0, 0))
    return pl.pallas_call(
        kernel,
        grid=(steps,),
        in_specs=[
            pl.BlockSpec((PAIR, MODES, 1), lambda n: (0, 0, 0)),
            pl.BlockSpec((1, tile), lambda n: (0, n + half * steps)),
        ]
        + [pl.BlockSpec((32, tile), lambda n: (0, n))] * GROUPS
        + [whole] * (before is not None),
        out_specs=whole,
        out_shape=jax.ShapeDtypeStruct((PAIR, 24, 128), F32),
        scratch_shapes=[pltpu.VMEM((PAIR, 80, 128), F32)],
        compiler_params=pltpu.CompilerParams(vmem_limit_bytes=SMALL),
        cost_estimate=pl.CostEstimate(
            flops=2 * PAIR * 64 * 256 * part, bytes_accessed=4 * 64 * part, transcendentals=0
        ),
        name="gram",
    )(pivot_local, weights, *pieces, *([] if before is None else [before]))


def split3(value):
    high = value.astype(BF16)
    rest = value - high.astype(F32)
    mid = rest.astype(BF16)
    low = (rest - mid.astype(F32)).astype(BF16)
    return high, mid, low


def right_side(cross):
    turn = turned(cross)
    first = low_rows(cross.shape)
    full = jnp.concatenate(
        [
            jnp.where(first, cross, other_rows(turn)),
            jnp.where(first, other_rows(cross), turn),
        ],
        axis=0,
    )
    full = jnp.concatenate([full, turned(full)], axis=1)
    high, mid, low = split3(full)
    return jnp.concatenate([high, mid, high, mid, low, high], axis=0)


def leading_basis(crosses, begin):
    count = len(crosses)
    rights = [right_side(cross) for cross in crosses]
    vec = jnp.stack([begin[0]] * count)
    alt = jnp.stack([begin[1]] * count)
    low_lane = low_lanes((MODES, 128))
    row = lax.broadcasted_iota(jnp.int32, (count, MODES, 1), 1)
    for _ in range(ITERS):
        new = []
        for f in range(count):
            high, mid, low = split3(vec[f])
            mixed = jnp.where(low_lane, high.astype(F32), low.astype(F32)).astype(BF16)
            left = jnp.concatenate([high, mid, mixed], axis=1)
            new.append(jnp.dot(left, rights[f], preferred_element_type=F32))
        new = jnp.stack(new)
        vec, alt = new[:, :, :128], new[:, :, 128:]
        scale = jnp.ones((count, MODES, 1), F32)
        for j in range(MODES):
            q = jnp.broadcast_to(vec[:, j : j + 1], vec.shape)
            q_alt = jnp.broadcast_to(alt[:, j : j + 1], vec.shape)
            power = jnp.sum(q * q, axis=2, keepdims=True)
            scale = jnp.where(row == j, lax.rsqrt(power * 0.5 + 1e-06), scale)
            if j < MODES - 1:
                inverse = jnp.where(row > j, 1.0 / (power + 2e-06), 0.0)
                coef_re = jnp.sum(vec * q, axis=2, keepdims=True) * inverse
                coef_im = jnp.sum(vec * q_alt, axis=2, keepdims=True) * inverse
                vec, alt = (
                    vec - (coef_re * q + coef_im * q_alt),
                    alt - (coef_re * q_alt - coef_im * q),
                )
        vec = vec * scale
        alt = alt * scale
    return vec, alt


def modes_call(pair, place, start, weights, degrees, sums, early, late, before, row_count, tile):
    rows_dev = weights.shape[1]
    steps = rows_dev // tile
    part_steps = steps // HALVES
    bands = tile * DEGREES // row_count

    def kernel(place_ref, start_ref, w_ref, deg_ref, sum_ref, *rest):
        x_refs, rest = rest[: HALVES * GROUPS], rest[HALVES * GROUPS :]
        modes_ref, energy_ref, expand, phase = rest[-4:]
        n = pl.program_id(0)

        @pl.when(n == 0)
        def _():
            total = jnp.sum(sum_ref[...], axis=0)
            crosses = []
            for f in range(PAIR):
                packed = total[f, :16] * (1.0 / row_count)
                swap = pltpu.roll(packed, 64, 1)
                low = low_lanes(packed.shape)
                crosses.append(
                    jnp.concatenate(
                        [jnp.where(low, packed, swap), jnp.where(low, swap, packed)], axis=0
                    )
                )
            vec, alt = leading_basis(crosses, start_ref[place_ref[0]])
            odd = odd_lanes(vec.shape)
            low = low_lanes(vec.shape)
            upper = jnp.where(odd, -vec, vec).astype(BF16).astype(F32)
            lower = jnp.where(odd, alt, -alt).astype(BF16).astype(F32)
            at = jnp.where(low, total[:, 16:24], 0.0)
            z_re = jnp.sum(upper * at, axis=2, keepdims=True)
            z_im = jnp.sum(lower * at, axis=2, keepdims=True)
            inverse = lax.rsqrt(z_re * z_re + z_im * z_im + 1.0)
            phase[0] = jnp.broadcast_to(z_re * inverse, vec.shape)
            phase[1] = jnp.broadcast_to(z_im * inverse, vec.shape)
            expand[:, :8] = upper
            expand[:, 8:] = lower
            energy_ref[...] = jnp.zeros_like(energy_ref) if before is None else rest[1][...]

        def tile_of(half):
            w = w_ref[...]
            lane = lax.broadcasted_iota(jnp.int32, (MODES, 128), 1)
            base = place_ref[1] + n * bands
            hits = [deg_ref[...] == base + m for m in range(bands + 1)]
            total = jnp.zeros((MODES, 128), F32)
            for f in range(PAIR):
                rows = slice(16 * f, 16 * f + 16)
                x = jnp.concatenate(
                    [r[rows] for r in x_refs[GROUPS * half : GROUPS * half + GROUPS]], axis=0
                )
                psi = jnp.dot(expand[f][:, :64].astype(BF16), x, preferred_element_type=F32)
                s_re = phase[0, f, :, :1]
                s_im = phase[1, f, :, :1]
                p_re, p_im = psi[:8], psi[8:]
                out_re = p_re * s_re + p_im * s_im
                out_im = p_im * s_re - p_re * s_im
                modes_ref[f, 0] = out_re.astype(BF16)
                modes_ref[f, 1] = out_im.astype(BF16)
                power = w * (out_re * out_re + out_im * out_im)
                for m in range(bands + 1):
                    level = jnp.sum(jnp.where(hits[m], power, 0.0), axis=1, keepdims=True)
                    spot = (pair * PAIR + f) * 32 + place_ref[2] + n * bands + m
                    total = total + jnp.where(lane == spot, level * (DEGREES / row_count), 0.0)
            energy_ref[...] += total

        for half in range(HALVES):
            pl.when(n // part_steps == half)(functools.partial(tile_of, half))

    in_specs = [
        pl.BlockSpec((GROUPS, 2, MODES, 128), lambda n, p: (0, 0, 0, 0)),
        pl.BlockSpec((1, tile), lambda n, p: (0, n)),
        pl.BlockSpec((1, tile), lambda n, p: (0, n)),
        pl.BlockSpec(sums.shape, lambda n, p: (0, 0, 0, 0)),
    ]
    in_specs += [
        pl.BlockSpec((32, tile), lambda n, p: (0, jnp.minimum(n, part_steps - 1)))
    ] * GROUPS
    in_specs += [
        pl.BlockSpec((32, tile), lambda n, p: (0, jnp.maximum(n - part_steps, 0)))
    ] * GROUPS
    args = [place, start, weights, degrees, sums, *early, *late]
    aliases = {}
    if before is not None:
        in_specs += [
            pl.BlockSpec(memory_space=pl.ANY),
            pl.BlockSpec((MODES, 128), lambda n, p: (0, 0)),
        ]
        aliases = {len(args): 0}
        args += list(before)
    return pl.pallas_call(
        kernel,
        grid_spec=pltpu.PrefetchScalarGridSpec(
            num_scalar_prefetch=1,
            grid=(steps,),
            in_specs=in_specs,
            out_specs=[
                pl.BlockSpec((PAIR, 2, MODES, tile), lambda n, p: (pair, 0, 0, n)),
                pl.BlockSpec((MODES, 128), lambda n, p: (0, 0)),
            ],
            scratch_shapes=[
                pltpu.VMEM((PAIR, 16, 128), F32),
                pltpu.VMEM((2, PAIR, MODES, 128), F32),
            ],
        ),
        out_shape=[
            jax.ShapeDtypeStruct((OWNED, 2, MODES, rows_dev), BF16),
            jax.ShapeDtypeStruct((MODES, 128), F32),
        ],
        input_output_aliases=aliases,
        compiler_params=pltpu.CompilerParams(vmem_limit_bytes=SMALL),
        cost_estimate=pl.CostEstimate(
            flops=2 * PAIR * 64 * 256 * rows_dev + 10**9,
            bytes_accessed=PAIR * 2 * 80 * rows_dev,
            transcendentals=0,
        ),
        name="modes",
    )(*args)


def energy_call(gathered):
    chips = gathered.shape[0]

    def kernel(in_ref, out_ref):
        out_ref[...] = jnp.zeros_like(out_ref)
        lane = lax.broadcasted_iota(jnp.int32, (MODES, 128), 1)
        for c in range(chips):
            value = in_ref[c]
            for f in range(OWNED):
                begin = c * 2 * LEVELS
                piece = jnp.where((lane >= 32 * f) & (lane < 32 * f + 2 * LEVELS + 1), value, 0.0)
                shift = (begin - 32 * f) % 128
                piece = pltpu.roll(piece, shift, 1) if shift else piece
                column = begin // 128
                split = 128 - begin % 128
                if split >= 2 * LEVELS + 1:
                    out_ref[f, :, column * 128 : column * 128 + 128] += piece
                else:
                    head = jnp.where(lane >= begin % 128, piece, 0.0)
                    out_ref[f, :, column * 128 : column * 128 + 128] += head
                    if (column + 1) * 128 < DEGREES:
                        out_ref[f, :, (column + 1) * 128 : (column + 2) * 128] += piece - head

    return pl.pallas_call(
        kernel,
        out_shape=jax.ShapeDtypeStruct((OWNED, MODES, DEGREES), F32),
        name="energy",
    )(gathered)


def gather_chips(value):
    value = value + lax.ppermute(value, "core", [(0, 1), (1, 0)])
    chips = STATE[0] * STATE[1]
    spread = jnp.broadcast_to(value[None], (chips,) + value.shape)
    return lax.all_to_all(spread, ("z", "x"), 0, 0, tiled=True)


def after(value, first):
    return lax.optimization_barrier((value, first))[0]


def per_device(snapshots, weights, degrees, pivots):
    rows_dev = snapshots.shape[2]
    row_count = rows_dev * DEVICES
    core = lax.axis_index("core").astype(jnp.int32)
    state = (lax.axis_index(("z", "x", "core"))).astype(jnp.int32)
    y = lax.axis_index("blk").astype(jnp.int32)
    place = jnp.stack([y, state * LEVELS, core * LEVELS])
    pivot_local = (pivots - state * rows_dev)[:, :, None]
    weights = weights.reshape(1, rows_dev)
    degrees = degrees.reshape(1, rows_dev)
    start = jnp.asarray(start_basis())

    halves = [spectra_call(snapshots, half, 2048) for half in range(HALVES)]
    pieces = {}
    for pair in range(PAIR):
        for half in range(HALVES):
            sent = halves[half][pair]
            pieces[pair, half] = [sent[0]] + [
                lax.ppermute(sent[k], "blk", [(g, (g + k) % GROUPS) for g in range(GROUPS)])
                for k in range(1, GROUPS)
            ]
    before = None
    for pair in range(PAIR):
        gram = None
        for half in range(HALVES):
            known = weights if before is None or half < HALVES - 1 else after(weights, before[1])
            gram = gram_call(
                half, pieces[pair, half], known, pivot_local[PAIR * pair : PAIR * pair + PAIR], gram, 4096
            )
        before = modes_call(
            pair, place, start, weights, degrees, gather_chips(gram),
            pieces[pair, 0], pieces[pair, 1], before, row_count, 4096,
        )
    modes, energy = before
    return modes, energy_call(gather_chips(energy))


def solution(mesh):
    fine = Mesh(mesh.devices.reshape(*STATE, GROUPS), ("z", "x", "core", "blk"))
    state = ("z", "x", "core")
    return jax.shard_map(
        per_device,
        mesh=fine,
        in_specs=(P("blk", None, state), P(state), P(state), P("blk", None)),
        out_specs=(P("blk", None, None, state), P("blk", None, None)),
        check_vma=False,
    )
```

```python
import functools
import math

import jax
import jax.numpy as jnp
import numpy as np
from jax import lax
from jax.experimental import pallas as pl
from jax.experimental.pallas import tpu as pltpu
from jax.sharding import Mesh
from jax.sharding import PartitionSpec as P

NF = 16
DEGREES = 384
ITERS = 6
MODES = 8
WINDOW = 64
GROUPS = 4
PER_GROUP = 8
QUAD = 4
OWNED = 4
PAIR = 2
HALVES = 2
BLOCKS = GROUPS * PER_GROUP
STATE = (4, 4, 2)
DEVICES = 32
LEVELS = DEGREES // DEVICES
F32 = jnp.float32
BF16 = jnp.bfloat16
LARGE = 60 * 1024 * 1024
SMALL = 24 * 1024 * 1024


def dft_table():
    t = np.arange(WINDOW, dtype=np.int32)
    order = np.arange(1, NF + 1, dtype=np.int32)
    two_pi = np.float32(2.0 * math.pi)
    window = np.float32(0.5) - np.float32(0.5) * np.cos(two_pi * t.astype(np.float32) / np.float32(WINDOW))
    norm = np.sqrt(np.sum(window * window))
    turns = order[:, None] * t[None, :] % WINDOW
    angle = two_pi * turns.astype(np.float32) / np.float32(WINDOW)
    table = np.stack([window * np.cos(angle) / norm, -window * np.sin(angle) / norm], axis=1)
    return table.astype(BF16)


def spectral_lhs():
    table = dft_table()
    lhs = np.zeros((GROUPS, OWNED, 2, QUAD, QUAD, WINDOW), dtype=BF16)
    for owner in range(GROUPS):
        for i in range(OWNED):
            for b in range(QUAD):
                lhs[owner, i, :, b, b, :] = table[OWNED * owner + i]
    return lhs.reshape(GROUPS, OWNED * 2 * QUAD, QUAD * WINDOW)


def start_basis():
    b = np.arange(BLOCKS, dtype=np.float32)
    j = np.arange(MODES, dtype=np.float32)
    v0 = np.cos(np.float32(math.pi) * (j[:, None] + np.float32(0.5)) * (b[None, :] + np.float32(0.5)) / np.float32(BLOCKS))
    v0 = (v0 * np.float32(math.sqrt(2.0 / BLOCKS))).reshape(MODES, GROUPS, 2, QUAD)
    out = np.zeros((GROUPS, 2, MODES, 2, GROUPS, 2, 2, QUAD), dtype=np.float32)
    for y in range(GROUPS):
        for slot in range(GROUPS):
            for part in range(2):
                out[y, part, :, :, slot, :, part, :] = v0[:, None, (y - slot) % GROUPS]
    return out.reshape(GROUPS, 2, MODES, 128)


def spectra_call(snapshots, half, tile):
    blocks_dev, window_len, rows_dev = snapshots.shape
    rows = OWNED * 2 * QUAD
    depth = QUAD * window_len
    part = rows_dev // HALVES
    steps = part // tile
    lhs_all = jnp.asarray(spectral_lhs())

    def kernel(lhs_ref, x_ref, *rest):
        outs, lhs = rest[:-1], rest[-1]

        @pl.when(pl.program_id(0) == 0)
        def _():
            for slot in range(GROUPS):
                owner = lax.rem(lax.axis_index("blk") + slot, GROUPS)
                lhs[slot * rows : (slot + 1) * rows, :] = lhs_ref[owner]

        data = x_ref[...].reshape(2, depth, tile)
        result = [jnp.dot(lhs[...], data[q], preferred_element_type=F32) for q in range(2)]
        for n, out in enumerate(outs):
            out[...] = jnp.concatenate(
                [
                    result[q][8 * m : 8 * m + 8]
                    for m in range(PAIR * n, PAIR * n + PAIR)
                    for q in range(2)
                ],
                axis=0,
            ).astype(BF16)

    out = pl.pallas_call(
        kernel,
        grid=(steps,),
        in_specs=[
            pl.BlockSpec((GROUPS, rows, depth), lambda n: (0, 0, 0)),
            pl.BlockSpec((blocks_dev, window_len, tile), lambda n: (0, 0, n + half * steps)),
        ],
        out_specs=[pl.BlockSpec((32, tile), lambda n: (0, n))] * (GROUPS * PAIR),
        scratch_shapes=[pltpu.VMEM((GROUPS * rows, depth), BF16)],
        out_shape=[jax.ShapeDtypeStruct((32, part), BF16)] * (GROUPS * PAIR),
        compiler_params=pltpu.CompilerParams(vmem_limit_bytes=LARGE),
        cost_estimate=pl.CostEstimate(
            flops=4 * GROUPS * rows * depth * part,
            bytes_accessed=4 * (depth + GROUPS * rows) * part,
            transcendentals=0,
        ),
        name="spectra",
    )(lhs_all, snapshots)
    return [[out[slot * PAIR + i] for slot in range(GROUPS)] for i in range(PAIR)]


def odd_lanes(shape):
    return (lax.broadcasted_iota(jnp.int32, shape, len(shape) - 1) & QUAD) == QUAD


def low_lanes(shape):
    return lax.broadcasted_iota(jnp.int32, shape, len(shape) - 1) < 64


def low_rows(shape):
    return lax.broadcasted_iota(jnp.int32, shape, len(shape) - 2) % 8 < QUAD


def other_lanes(value):
    axis = value.ndim - 1
    return jnp.where(
        odd_lanes(value.shape), pltpu.roll(value, QUAD, axis), pltpu.roll(value, 128 - QUAD, axis)
    )


def other_rows(value):
    rows = value.shape[0]
    return pltpu.roll(value.reshape(rows // 8, 8, 128), QUAD, 1).reshape(rows, 128)


def turned(value):
    other = other_lanes(value)
    return jnp.where(odd_lanes(value.shape), other, -other)


def gram_call(half, pieces, weights, pivot_local, before, tile):
    part = pieces[0].shape[1]
    steps = part // tile

    def kernel(p_ref, w_ref, *rest):
        x_refs, rest = rest[:GROUPS], rest[GROUPS:]
        out_ref, acc = rest[-2:]
        n = pl.program_id(0)

        @pl.when(n == 0)
        def _():
            acc[...] = jnp.zeros_like(acc)

        lane = lax.broadcasted_iota(jnp.int32, (MODES, tile), 1) + (n + half * steps) * tile
        for f in range(PAIR):
            x = jnp.concatenate([r[16 * f : 16 * f + 16] for r in x_refs], axis=0)
            wx = x.astype(F32) * w_ref[...]
            hot = jnp.where(lane == p_ref[f], 1.0, 0.0)
            left = jnp.concatenate([wx, hot, jnp.zeros_like(hot)], axis=0).astype(BF16)
            acc[f, :, :64] += lax.dot_general(
                left, x, (((1,), (1,)), ((), ())), preferred_element_type=F32
            )

        @pl.when(n == steps - 1)
        def _():
            for f in range(PAIR):
                total = acc[f]
                total = total + pltpu.roll(total, 64, 1)
                gram = total[:64]
                same = low_rows(gram.shape) != odd_lanes(gram.shape)
                cross = other_lanes(other_rows(gram)) + jnp.where(same, gram, -gram)
                cross = jnp.where(low_rows((32, 128)), cross[:32], other_rows(cross[32:]))
                packed = jnp.where(low_lanes((16, 128)), cross[:16], cross[16:])
                packed = jnp.concatenate([packed, total[64:72]], axis=0)
                if before is not None:
                    packed = packed + rest[0][f]
                out_ref[f] = packed

    whole = pl.BlockSpec((PAIR, 24, 128), lambda n: (0, 0, 0))
    return pl.pallas_call(
        kernel,
        grid=(steps,),
        in_specs=[
            pl.BlockSpec((PAIR, MODES, 1), lambda n: (0, 0, 0)),
            pl.BlockSpec((1, tile), lambda n: (0, n + half * steps)),
        ]
        + [pl.BlockSpec((32, tile), lambda n: (0, n))] * GROUPS
        + [whole] * (before is not None),
        out_specs=whole,
        out_shape=jax.ShapeDtypeStruct((PAIR, 24, 128), F32),
        scratch_shapes=[pltpu.VMEM((PAIR, 80, 128), F32)],
        compiler_params=pltpu.CompilerParams(vmem_limit_bytes=SMALL),
        cost_estimate=pl.CostEstimate(
            flops=2 * PAIR * 64 * 256 * part, bytes_accessed=4 * 64 * part, transcendentals=0
        ),
        name="gram",
    )(pivot_local, weights, *pieces, *([] if before is None else [before]))


def split3(value):
    high = value.astype(BF16)
    rest = value - high.astype(F32)
    mid = rest.astype(BF16)
    low = (rest - mid.astype(F32)).astype(BF16)
    return high, mid, low


def right_side(cross):
    turn = turned(cross)
    first = low_rows(cross.shape)
    full = jnp.concatenate(
        [
            jnp.where(first, cross, other_rows(turn)),
            jnp.where(first, other_rows(cross), turn),
        ],
        axis=0,
    )
    full = jnp.concatenate([full, turned(full)], axis=1)
    high, mid, low = split3(full)
    return jnp.concatenate([high, mid, high, mid, low, high], axis=0)


def leading_basis(crosses, begin):
    count = len(crosses)
    rights = [right_side(cross) for cross in crosses]
    vec = jnp.stack([begin[0]] * count)
    alt = jnp.stack([begin[1]] * count)
    low_lane = low_lanes((MODES, 128))
    row = lax.broadcasted_iota(jnp.int32, (count, MODES, 1), 1)
    for _ in range(ITERS):
        new = []
        for f in range(count):
            high, mid, low = split3(vec[f])
            mixed = jnp.where(low_lane, high.astype(F32), low.astype(F32)).astype(BF16)
            left = jnp.concatenate([high, mid, mixed], axis=1)
            new.append(jnp.dot(left, rights[f], preferred_element_type=F32))
        new = jnp.stack(new)
        vec, alt = new[:, :, :128], new[:, :, 128:]
        scale = jnp.ones((count, MODES, 1), F32)
        for j in range(MODES):
            q = jnp.broadcast_to(vec[:, j : j + 1], vec.shape)
            q_alt = jnp.broadcast_to(alt[:, j : j + 1], vec.shape)
            power = jnp.sum(q * q, axis=2, keepdims=True)
            scale = jnp.where(row == j, lax.rsqrt(power * 0.5 + 1e-06), scale)
            if j < MODES - 1:
                inverse = jnp.where(row > j, 1.0 / (power + 2e-06), 0.0)
                coef_re = jnp.sum(vec * q, axis=2, keepdims=True) * inverse
                coef_im = jnp.sum(vec * q_alt, axis=2, keepdims=True) * inverse
                vec, alt = (
                    vec - (coef_re * q + coef_im * q_alt),
                    alt - (coef_re * q_alt - coef_im * q),
                )
        vec = vec * scale
        alt = alt * scale
    return vec, alt


def modes_call(pair, place, start, weights, degrees, sums, early, late, before, row_count, tile):
    rows_dev = weights.shape[1]
    steps = rows_dev // tile
    part_steps = steps // HALVES
    bands = tile * DEGREES // row_count

    def kernel(place_ref, start_ref, w_ref, deg_ref, sum_ref, *rest):
        x_refs, rest = rest[: HALVES * GROUPS], rest[HALVES * GROUPS :]
        modes_ref, energy_ref, expand, phase = rest[-4:]
        n = pl.program_id(0)

        @pl.when(n == 0)
        def _():
            total = jnp.sum(sum_ref[...], axis=0)
            crosses = []
            for f in range(PAIR):
                packed = total[f, :16] * (1.0 / row_count)
                swap = pltpu.roll(packed, 64, 1)
                low = low_lanes(packed.shape)
                crosses.append(
                    jnp.concatenate(
                        [jnp.where(low, packed, swap), jnp.where(low, swap, packed)], axis=0
                    )
                )
            vec, alt = leading_basis(crosses, start_ref[place_ref[0]])
            odd = odd_lanes(vec.shape)
            low = low_lanes(vec.shape)
            upper = jnp.where(odd, -vec, vec).astype(BF16).astype(F32)
            lower = jnp.where(odd, alt, -alt).astype(BF16).astype(F32)
            at = jnp.where(low, total[:, 16:24], 0.0)
            z_re = jnp.sum(upper * at, axis=2, keepdims=True)
            z_im = jnp.sum(lower * at, axis=2, keepdims=True)
            inverse = lax.rsqrt(z_re * z_re + z_im * z_im + 1.0)
            phase[0] = jnp.broadcast_to(z_re * inverse, vec.shape)
            phase[1] = jnp.broadcast_to(z_im * inverse, vec.shape)
            expand[:, :8] = upper
            expand[:, 8:] = lower
            energy_ref[...] = jnp.zeros_like(energy_ref) if before is None else rest[1][...]

        def tile_of(half):
            w = w_ref[...]
            lane = lax.broadcasted_iota(jnp.int32, (MODES, 128), 1)
            base = place_ref[1] + n * bands
            hits = [deg_ref[...] == base + m for m in range(bands + 1)]
            total = jnp.zeros((MODES, 128), F32)
            for f in range(PAIR):
                rows = slice(16 * f, 16 * f + 16)
                x = jnp.concatenate(
                    [r[rows] for r in x_refs[GROUPS * half : GROUPS * half + GROUPS]], axis=0
                )
                psi = jnp.dot(expand[f][:, :64].astype(BF16), x, preferred_element_type=F32)
                s_re = phase[0, f, :, :1]
                s_im = phase[1, f, :, :1]
                p_re, p_im = psi[:8], psi[8:]
                out_re = p_re * s_re + p_im * s_im
                out_im = p_im * s_re - p_re * s_im
                modes_ref[f, 0] = out_re.astype(BF16)
                modes_ref[f, 1] = out_im.astype(BF16)
                power = w * (out_re * out_re + out_im * out_im)
                for m in range(bands + 1):
                    level = jnp.sum(jnp.where(hits[m], power, 0.0), axis=1, keepdims=True)
                    spot = (pair * PAIR + f) * 32 + place_ref[2] + n * bands + m
                    total = total + jnp.where(lane == spot, level * (DEGREES / row_count), 0.0)
            energy_ref[...] += total

        for half in range(HALVES):
            pl.when(n // part_steps == half)(functools.partial(tile_of, half))

    in_specs = [
        pl.BlockSpec((GROUPS, 2, MODES, 128), lambda n, p: (0, 0, 0, 0)),
        pl.BlockSpec((1, tile), lambda n, p: (0, n)),
        pl.BlockSpec((1, tile), lambda n, p: (0, n)),
        pl.BlockSpec(sums.shape, lambda n, p: (0, 0, 0, 0)),
    ]
    in_specs += [
        pl.BlockSpec((32, tile), lambda n, p: (0, jnp.minimum(n, part_steps - 1)))
    ] * GROUPS
    in_specs += [
        pl.BlockSpec((32, tile), lambda n, p: (0, jnp.maximum(n - part_steps, 0)))
    ] * GROUPS
    args = [place, start, weights, degrees, sums, *early, *late]
    aliases = {}
    if before is not None:
        in_specs += [
            pl.BlockSpec(memory_space=pl.ANY),
            pl.BlockSpec((MODES, 128), lambda n, p: (0, 0)),
        ]
        aliases = {len(args): 0}
        args += list(before)
    return pl.pallas_call(
        kernel,
        grid_spec=pltpu.PrefetchScalarGridSpec(
            num_scalar_prefetch=1,
            grid=(steps,),
            in_specs=in_specs,
            out_specs=[
                pl.BlockSpec((PAIR, 2, MODES, tile), lambda n, p: (pair, 0, 0, n)),
                pl.BlockSpec((MODES, 128), lambda n, p: (0, 0)),
            ],
            scratch_shapes=[
                pltpu.VMEM((PAIR, 16, 128), F32),
                pltpu.VMEM((2, PAIR, MODES, 128), F32),
            ],
        ),
        out_shape=[
            jax.ShapeDtypeStruct((OWNED, 2, MODES, rows_dev), BF16),
            jax.ShapeDtypeStruct((MODES, 128), F32),
        ],
        input_output_aliases=aliases,
        compiler_params=pltpu.CompilerParams(vmem_limit_bytes=SMALL),
        cost_estimate=pl.CostEstimate(
            flops=2 * PAIR * 64 * 256 * rows_dev + 10**9,
            bytes_accessed=PAIR * 2 * 80 * rows_dev,
            transcendentals=0,
        ),
        name="modes",
    )(*args)


def energy_call(gathered):
    chips = gathered.shape[0]

    def kernel(in_ref, out_ref):
        out_ref[...] = jnp.zeros_like(out_ref)
        lane = lax.broadcasted_iota(jnp.int32, (MODES, 128), 1)
        for c in range(chips):
            value = in_ref[c]
            for f in range(OWNED):
                begin = c * 2 * LEVELS
                piece = jnp.where((lane >= 32 * f) & (lane < 32 * f + 2 * LEVELS + 1), value, 0.0)
                shift = (begin - 32 * f) % 128
                piece = pltpu.roll(piece, shift, 1) if shift else piece
                column = begin // 128
                split = 128 - begin % 128
                if split >= 2 * LEVELS + 1:
                    out_ref[f, :, column * 128 : column * 128 + 128] += piece
                else:
                    head = jnp.where(lane >= begin % 128, piece, 0.0)
                    out_ref[f, :, column * 128 : column * 128 + 128] += head
                    if (column + 1) * 128 < DEGREES:
                        out_ref[f, :, (column + 1) * 128 : (column + 2) * 128] += piece - head

    return pl.pallas_call(
        kernel,
        out_shape=jax.ShapeDtypeStruct((OWNED, MODES, DEGREES), F32),
        name="energy",
    )(gathered)


def gather_chips(value):
    value = value + lax.ppermute(value, "core", [(0, 1), (1, 0)])
    chips = STATE[0] * STATE[1]
    spread = jnp.broadcast_to(value[None], (chips,) + value.shape)
    return lax.all_to_all(spread, ("z", "x"), 0, 0, tiled=True)


def after(value, first):
    return lax.optimization_barrier((value, first))[0]


def per_device(snapshots, weights, degrees, pivots):
    rows_dev = snapshots.shape[2]
    row_count = rows_dev * DEVICES
    core = lax.axis_index("core").astype(jnp.int32)
    state = (lax.axis_index(("z", "x", "core"))).astype(jnp.int32)
    y = lax.axis_index("blk").astype(jnp.int32)
    place = jnp.stack([y, state * LEVELS, core * LEVELS])
    pivot_local = (pivots - state * rows_dev)[:, :, None]
    weights = weights.reshape(1, rows_dev)
    degrees = degrees.reshape(1, rows_dev)
    start = jnp.asarray(start_basis())

    halves = [spectra_call(snapshots, half, 4096) for half in range(HALVES)]
    pieces = {}
    for pair in range(PAIR):
        for half in range(HALVES):
            sent = halves[half][pair]
            pieces[pair, half] = [sent[0]] + [
                lax.ppermute(sent[k], "blk", [(g, (g + k) % GROUPS) for g in range(GROUPS)])
                for k in range(1, GROUPS)
            ]
    before = None
    for pair in range(PAIR):
        gram = None
        for half in range(HALVES):
            known = weights if before is None or half < HALVES - 1 else after(weights, before[1])
            gram = gram_call(
                half, pieces[pair, half], known, pivot_local[PAIR * pair : PAIR * pair + PAIR], gram, 8192
            )
        before = modes_call(
            pair, place, start, weights, degrees, gather_chips(gram),
            pieces[pair, 0], pieces[pair, 1], before, row_count, 8192,
        )
    modes, energy = before
    return modes, energy_call(gather_chips(energy))


def solution(mesh):
    fine = Mesh(mesh.devices.reshape(*STATE, GROUPS), ("z", "x", "core", "blk"))
    state = ("z", "x", "core")
    return jax.shard_map(
        per_device,
        mesh=fine,
        in_specs=(P("blk", None, state), P(state), P(state), P("blk", None)),
        out_specs=(P("blk", None, None, state), P("blk", None, None)),
        check_vma=False,
    )
```

```python
import functools
import math

import jax
import jax.numpy as jnp
import numpy as np
from jax import lax
from jax.experimental import pallas as pl
from jax.experimental.pallas import tpu as pltpu
from jax.sharding import Mesh
from jax.sharding import PartitionSpec as P

NF = 16
DEGREES = 384
ITERS = 6
MODES = 8
WINDOW = 64
GROUPS = 4
PER_GROUP = 8
QUAD = 4
OWNED = 4
PAIR = 2
HALVES = 2
BLOCKS = GROUPS * PER_GROUP
STATE = (4, 4, 2)
DEVICES = 32
LEVELS = DEGREES // DEVICES
F32 = jnp.float32
BF16 = jnp.bfloat16
LARGE = 60 * 1024 * 1024
SMALL = 24 * 1024 * 1024


def dft_table():
    t = np.arange(WINDOW, dtype=np.int32)
    order = np.arange(1, NF + 1, dtype=np.int32)
    two_pi = np.float32(2.0 * math.pi)
    window = np.float32(0.5) - np.float32(0.5) * np.cos(two_pi * t.astype(np.float32) / np.float32(WINDOW))
    norm = np.sqrt(np.sum(window * window))
    turns = order[:, None] * t[None, :] % WINDOW
    angle = two_pi * turns.astype(np.float32) / np.float32(WINDOW)
    table = np.stack([window * np.cos(angle) / norm, -window * np.sin(angle) / norm], axis=1)
    return table.astype(BF16)


def spectral_lhs():
    table = dft_table()
    lhs = np.zeros((GROUPS, OWNED, 2, QUAD, QUAD, WINDOW), dtype=BF16)
    for owner in range(GROUPS):
        for i in range(OWNED):
            for b in range(QUAD):
                lhs[owner, i, :, b, b, :] = table[OWNED * owner + i]
    return lhs.reshape(GROUPS, OWNED * 2 * QUAD, QUAD * WINDOW)


def start_basis():
    b = np.arange(BLOCKS, dtype=np.float32)
    j = np.arange(MODES, dtype=np.float32)
    v0 = np.cos(np.float32(math.pi) * (j[:, None] + np.float32(0.5)) * (b[None, :] + np.float32(0.5)) / np.float32(BLOCKS))
    v0 = (v0 * np.float32(math.sqrt(2.0 / BLOCKS))).reshape(MODES, GROUPS, 2, QUAD)
    out = np.zeros((GROUPS, 2, MODES, 2, GROUPS, 2, 2, QUAD), dtype=np.float32)
    for y in range(GROUPS):
        for slot in range(GROUPS):
            for part in range(2):
                out[y, part, :, :, slot, :, part, :] = v0[:, None, (y - slot) % GROUPS]
    return out.reshape(GROUPS, 2, MODES, 128)


def spectra_call(snapshots, half, tile):
    blocks_dev, window_len, rows_dev = snapshots.shape
    rows = OWNED * 2 * QUAD
    depth = QUAD * window_len
    part = rows_dev // HALVES
    steps = part // tile
    lhs_all = jnp.asarray(spectral_lhs())

    def kernel(lhs_ref, x_ref, *rest):
        outs, lhs = rest[:-1], rest[-1]

        @pl.when(pl.program_id(0) == 0)
        def _():
            for slot in range(GROUPS):
                owner = lax.rem(lax.axis_index("blk") + slot, GROUPS)
                lhs[slot * rows : (slot + 1) * rows, :] = lhs_ref[owner]

        data = x_ref[...].reshape(2, depth, tile)
        result = [jnp.dot(lhs[...], data[q], preferred_element_type=F32) for q in range(2)]
        for n, out in enumerate(outs):
            out[...] = jnp.concatenate(
                [
                    result[q][8 * m : 8 * m + 8]
                    for m in range(PAIR * n, PAIR * n + PAIR)
                    for q in range(2)
                ],
                axis=0,
            ).astype(BF16)

    out = pl.pallas_call(
        kernel,
        grid=(steps,),
        in_specs=[
            pl.BlockSpec((GROUPS, rows, depth), lambda n: (0, 0, 0)),
            pl.BlockSpec((blocks_dev, window_len, tile), lambda n: (0, 0, n + half * steps)),
        ],
        out_specs=[pl.BlockSpec((32, tile), lambda n: (0, n))] * (GROUPS * PAIR),
        scratch_shapes=[pltpu.VMEM((GROUPS * rows, depth), BF16)],
        out_shape=[jax.ShapeDtypeStruct((32, part), BF16)] * (GROUPS * PAIR),
        compiler_params=pltpu.CompilerParams(vmem_limit_bytes=LARGE),
        cost_estimate=pl.CostEstimate(
            flops=4 * GROUPS * rows * depth * part,
            bytes_accessed=4 * (depth + GROUPS * rows) * part,
            transcendentals=0,
        ),
        name="spectra",
    )(lhs_all, snapshots)
    return [[out[slot * PAIR + i] for slot in range(GROUPS)] for i in range(PAIR)]


def odd_lanes(shape):
    return (lax.broadcasted_iota(jnp.int32, shape, len(shape) - 1) & QUAD) == QUAD


def low_lanes(shape):
    return lax.broadcasted_iota(jnp.int32, shape, len(shape) - 1) < 64


def low_rows(shape):
    return lax.broadcasted_iota(jnp.int32, shape, len(shape) - 2) % 8 < QUAD


def other_lanes(value):
    axis = value.ndim - 1
    return jnp.where(
        odd_lanes(value.shape), pltpu.roll(value, QUAD, axis), pltpu.roll(value, 128 - QUAD, axis)
    )


def other_rows(value):
    rows = value.shape[0]
    return pltpu.roll(value.reshape(rows // 8, 8, 128), QUAD, 1).reshape(rows, 128)


def turned(value):
    other = other_lanes(value)
    return jnp.where(odd_lanes(value.shape), other, -other)


def gram_call(half, pieces, weights, pivot_local, before):
    part = pieces[0].shape[1]

    def kernel(p_ref, w_ref, *rest):
        x_refs, rest = rest[:GROUPS], rest[GROUPS:]
        out_ref = rest[-1]
        lane = lax.broadcasted_iota(jnp.int32, (MODES, part), 1) + half * part
        for f in range(PAIR):
            x = jnp.concatenate([r[16 * f : 16 * f + 16] for r in x_refs], axis=0)
            wx = x.astype(F32) * w_ref[:, half * part : (half + 1) * part]
            hot = jnp.where(lane == p_ref[f], 1.0, 0.0)
            left = jnp.concatenate([wx, hot, jnp.zeros_like(hot)], axis=0).astype(BF16)
            total = lax.dot_general(left, x, (((1,), (1,)), ((), ())), preferred_element_type=F32)
            total = jnp.concatenate([total, total], axis=1)
            gram = total[:64]
            same = low_rows(gram.shape) != odd_lanes(gram.shape)
            cross = other_lanes(other_rows(gram)) + jnp.where(same, gram, -gram)
            cross = jnp.where(low_rows((32, 128)), cross[:32], other_rows(cross[32:]))
            packed = jnp.where(low_lanes((16, 128)), cross[:16], cross[16:])
            packed = jnp.concatenate([packed, total[64:72]], axis=0)
            if before is not None:
                packed = packed + rest[0][f]
            out_ref[f] = packed

    return pl.pallas_call(
        kernel,
        out_shape=jax.ShapeDtypeStruct((PAIR, 24, 128), F32),
        compiler_params=pltpu.CompilerParams(vmem_limit_bytes=SMALL),
        cost_estimate=pl.CostEstimate(
            flops=2 * PAIR * 64 * 256 * part, bytes_accessed=4 * 64 * part, transcendentals=0
        ),
        name="gram",
    )(pivot_local, weights, *pieces, *([] if before is None else [before]))


def split3(value):
    high = value.astype(BF16)
    rest = value - high.astype(F32)
    mid = rest.astype(BF16)
    low = (rest - mid.astype(F32)).astype(BF16)
    return high, mid, low


def right_side(cross):
    turn = turned(cross)
    first = low_rows(cross.shape)
    full = jnp.concatenate(
        [
            jnp.where(first, cross, other_rows(turn)),
            jnp.where(first, other_rows(cross), turn),
        ],
        axis=0,
    )
    full = jnp.concatenate([full, turned(full)], axis=1)
    high, mid, low = split3(full)
    return jnp.concatenate([high, mid, high, mid, low, high], axis=0)


def leading_basis(crosses, begin):
    count = len(crosses)
    rights = [right_side(cross) for cross in crosses]
    vec = jnp.stack([begin[0]] * count)
    alt = jnp.stack([begin[1]] * count)
    low_lane = low_lanes((MODES, 128))
    row = lax.broadcasted_iota(jnp.int32, (count, MODES, 1), 1)
    for _ in range(ITERS):
        new = []
        for f in range(count):
            high, mid, low = split3(vec[f])
            mixed = jnp.where(low_lane, high.astype(F32), low.astype(F32)).astype(BF16)
            left = jnp.concatenate([high, mid, mixed], axis=1)
            new.append(jnp.dot(left, rights[f], preferred_element_type=F32))
        new = jnp.stack(new)
        vec, alt = new[:, :, :128], new[:, :, 128:]
        scale = jnp.ones((count, MODES, 1), F32)
        for j in range(MODES):
            q = jnp.broadcast_to(vec[:, j : j + 1], vec.shape)
            q_alt = jnp.broadcast_to(alt[:, j : j + 1], vec.shape)
            power = jnp.sum(q * q, axis=2, keepdims=True)
            scale = jnp.where(row == j, lax.rsqrt(power * 0.5 + 1e-06), scale)
            if j < MODES - 1:
                inverse = jnp.where(row > j, 1.0 / (power + 2e-06), 0.0)
                coef_re = jnp.sum(vec * q, axis=2, keepdims=True) * inverse
                coef_im = jnp.sum(vec * q_alt, axis=2, keepdims=True) * inverse
                vec, alt = (
                    vec - (coef_re * q + coef_im * q_alt),
                    alt - (coef_re * q_alt - coef_im * q),
                )
        vec = vec * scale
        alt = alt * scale
    return vec, alt


def modes_call(pair, place, start, weights, degrees, sums, early, late, before, row_count):
    rows_dev = weights.shape[1]
    tile = rows_dev // HALVES
    bands = tile * DEGREES // row_count

    def kernel(place_ref, start_ref, w_ref, deg_ref, sum_ref, *rest):
        x_refs, rest = rest[: HALVES * GROUPS], rest[HALVES * GROUPS :]
        modes_ref, energy_ref, stage, sems = rest[-4:]
        total = jnp.sum(sum_ref[...], axis=0)
        crosses = []
        for f in range(PAIR):
            packed = total[f, :16] * (1.0 / row_count)
            swap = pltpu.roll(packed, 64, 1)
            low = low_lanes(packed.shape)
            crosses.append(
                jnp.concatenate(
                    [jnp.where(low, packed, swap), jnp.where(low, swap, packed)], axis=0
                )
            )
        vec, alt = leading_basis(crosses, start_ref[place_ref[0]])
        odd = odd_lanes(vec.shape)
        low = low_lanes(vec.shape)
        upper = jnp.where(odd, -vec, vec).astype(BF16).astype(F32)
        lower = jnp.where(odd, alt, -alt).astype(BF16).astype(F32)
        at = jnp.where(low, total[:, 16:24], 0.0)
        z_re = jnp.sum(upper * at, axis=2, keepdims=True)
        z_im = jnp.sum(lower * at, axis=2, keepdims=True)
        inverse = lax.rsqrt(z_re * z_re + z_im * z_im + 1.0)
        s_re = z_re * inverse
        s_im = z_im * inverse
        expand = jnp.concatenate([upper, lower], axis=1).astype(BF16)
        total = jnp.zeros((MODES, 128), F32) if before is None else rest[1][...]

        lane = lax.broadcasted_iota(jnp.int32, (MODES, 128), 1)
        copies = []
        for half in range(HALVES):
            span = slice(half * tile, (half + 1) * tile)
            w = w_ref[:, span]
            level_of = deg_ref[:, span]
            base = place_ref[1] + half * bands
            hits = [level_of == base + m for m in range(bands + 1)]
            for f in range(PAIR):
                rows = slice(16 * f, 16 * f + 16)
                x = jnp.concatenate(
                    [r[rows] for r in x_refs[GROUPS * half : GROUPS * half + GROUPS]], axis=0
                )
                psi = jnp.dot(expand[f][:, :64], x, preferred_element_type=F32)
                p_re, p_im = psi[:8], psi[8:]
                out_re = p_re * s_re[f] + p_im * s_im[f]
                out_im = p_im * s_re[f] - p_re * s_im[f]
                stage[half, f, 0] = out_re.astype(BF16)
                stage[half, f, 1] = out_im.astype(BF16)
                power = w * (out_re * out_re + out_im * out_im)
                for m in range(bands + 1):
                    level = jnp.sum(jnp.where(hits[m], power, 0.0), axis=1, keepdims=True)
                    spot = (pair * PAIR + f) * 32 + place_ref[2] + half * bands + m
                    total = total + jnp.where(lane == spot, level * (DEGREES / row_count), 0.0)
            copy = pltpu.make_async_copy(
                stage.at[half],
                modes_ref.at[pl.ds(pair * PAIR, PAIR), :, :, pl.ds(half * tile, tile)],
                sems.at[half],
            )
            copy.start()
            copies.append(copy)
        energy_ref[...] = total
        for copy in copies:
            copy.wait()

    vmem = pl.BlockSpec(memory_space=pltpu.VMEM)
    raw = pl.BlockSpec(memory_space=pl.ANY)
    args = [place, start, weights, degrees, sums, *early, *late]
    in_specs = [pl.BlockSpec(memory_space=pltpu.SMEM)] + [vmem] * (len(args) - 1)
    aliases = {}
    if before is not None:
        in_specs += [raw, vmem]
        aliases = {len(args): 0}
        args += list(before)
    return pl.pallas_call(
        kernel,
        in_specs=in_specs,
        out_specs=[raw, vmem],
        scratch_shapes=[
            pltpu.VMEM((HALVES, PAIR, 2, MODES, tile), BF16),
            pltpu.SemaphoreType.DMA((HALVES,)),
        ],
        out_shape=[
            jax.ShapeDtypeStruct((OWNED, 2, MODES, rows_dev), BF16),
            jax.ShapeDtypeStruct((MODES, 128), F32),
        ],
        input_output_aliases=aliases,
        compiler_params=pltpu.CompilerParams(vmem_limit_bytes=SMALL),
        cost_estimate=pl.CostEstimate(
            flops=2 * PAIR * 64 * 256 * rows_dev + 10**9,
            bytes_accessed=PAIR * 2 * 80 * rows_dev,
            transcendentals=0,
        ),
        name="modes",
    )(*args)


def energy_call(gathered):
    chips = gathered.shape[0]

    def kernel(in_ref, out_ref):
        out_ref[...] = jnp.zeros_like(out_ref)
        lane = lax.broadcasted_iota(jnp.int32, (MODES, 128), 1)
        for c in range(chips):
            value = in_ref[c]
            for f in range(OWNED):
                begin = c * 2 * LEVELS
                piece = jnp.where((lane >= 32 * f) & (lane < 32 * f + 2 * LEVELS + 1), value, 0.0)
                shift = (begin - 32 * f) % 128
                piece = pltpu.roll(piece, shift, 1) if shift else piece
                column = begin // 128
                split = 128 - begin % 128
                if split >= 2 * LEVELS + 1:
                    out_ref[f, :, column * 128 : column * 128 + 128] += piece
                else:
                    head = jnp.where(lane >= begin % 128, piece, 0.0)
                    out_ref[f, :, column * 128 : column * 128 + 128] += head
                    if (column + 1) * 128 < DEGREES:
                        out_ref[f, :, (column + 1) * 128 : (column + 2) * 128] += piece - head

    return pl.pallas_call(
        kernel,
        out_shape=jax.ShapeDtypeStruct((OWNED, MODES, DEGREES), F32),
        name="energy",
    )(gathered)


def gather_chips(value):
    value = value + lax.ppermute(value, "core", [(0, 1), (1, 0)])
    chips = STATE[0] * STATE[1]
    spread = jnp.broadcast_to(value[None], (chips,) + value.shape)
    return lax.all_to_all(spread, ("z", "x"), 0, 0, tiled=True)


def after(value, first):
    return lax.optimization_barrier((value, first))[0]


def per_device(snapshots, weights, degrees, pivots):
    rows_dev = snapshots.shape[2]
    row_count = rows_dev * DEVICES
    core = lax.axis_index("core").astype(jnp.int32)
    state = (lax.axis_index(("z", "x", "core"))).astype(jnp.int32)
    y = lax.axis_index("blk").astype(jnp.int32)
    place = jnp.stack([y, state * LEVELS, core * LEVELS])
    pivot_local = (pivots - state * rows_dev)[:, :, None]
    weights = weights.reshape(1, rows_dev)
    degrees = degrees.reshape(1, rows_dev)
    start = jnp.asarray(start_basis())

    halves = [spectra_call(snapshots, half, 4096) for half in range(HALVES)]
    pieces = {}
    for pair in range(PAIR):
        for half in range(HALVES):
            sent = halves[half][pair]
            pieces[pair, half] = [sent[0]] + [
                lax.ppermute(sent[k], "blk", [(g, (g + k) % GROUPS) for g in range(GROUPS)])
                for k in range(1, GROUPS)
            ]
    before = None
    for pair in range(PAIR):
        gram = None
        for half in range(HALVES):
            known = weights if before is None or half < HALVES - 1 else after(weights, before[1])
            gram = gram_call(
                half, pieces[pair, half], known, pivot_local[PAIR * pair : PAIR * pair + PAIR], gram
            )
        before = modes_call(
            pair, place, start, weights, degrees, gather_chips(gram),
            pieces[pair, 0], pieces[pair, 1], before, row_count,
        )
    modes, energy = before
    return modes, energy_call(gather_chips(energy))


def solution(mesh):
    fine = Mesh(mesh.devices.reshape(*STATE, GROUPS), ("z", "x", "core", "blk"))
    state = ("z", "x", "core")
    return jax.shard_map(
        per_device,
        mesh=fine,
        in_specs=(P("blk", None, state), P(state), P(state), P("blk", None)),
        out_specs=(P("blk", None, None, state), P("blk", None, None)),
        check_vma=False,
    )
```

```python
import functools
import math

import jax
import jax.numpy as jnp
import numpy as np
from jax import lax
from jax.experimental import pallas as pl
from jax.experimental.pallas import tpu as pltpu
from jax.sharding import Mesh
from jax.sharding import PartitionSpec as P

NF = 16
DEGREES = 384
ITERS = 6
MODES = 8
WINDOW = 64
GROUPS = 4
PER_GROUP = 8
QUAD = 4
OWNED = 4
PAIR = 2
HALVES = 2
BLOCKS = GROUPS * PER_GROUP
STATE = (4, 4, 2)
DEVICES = 32
LEVELS = DEGREES // DEVICES
F32 = jnp.float32
BF16 = jnp.bfloat16
LARGE = 60 * 1024 * 1024
SMALL = 24 * 1024 * 1024


def dft_table():
    t = np.arange(WINDOW, dtype=np.int32)
    order = np.arange(1, NF + 1, dtype=np.int32)
    two_pi = np.float32(2.0 * math.pi)
    window = np.float32(0.5) - np.float32(0.5) * np.cos(two_pi * t.astype(np.float32) / np.float32(WINDOW))
    norm = np.sqrt(np.sum(window * window))
    turns = order[:, None] * t[None, :] % WINDOW
    angle = two_pi * turns.astype(np.float32) / np.float32(WINDOW)
    table = np.stack([window * np.cos(angle) / norm, -window * np.sin(angle) / norm], axis=1)
    return table.astype(BF16)


def spectral_lhs():
    table = dft_table()
    lhs = np.zeros((GROUPS, OWNED, 2, QUAD, QUAD, WINDOW), dtype=BF16)
    for owner in range(GROUPS):
        for i in range(OWNED):
            for b in range(QUAD):
                lhs[owner, i, :, b, b, :] = table[OWNED * owner + i]
    return lhs.reshape(GROUPS, OWNED * 2 * QUAD, QUAD * WINDOW)


def start_basis():
    b = np.arange(BLOCKS, dtype=np.float32)
    j = np.arange(MODES, dtype=np.float32)
    v0 = np.cos(np.float32(math.pi) * (j[:, None] + np.float32(0.5)) * (b[None, :] + np.float32(0.5)) / np.float32(BLOCKS))
    v0 = (v0 * np.float32(math.sqrt(2.0 / BLOCKS))).reshape(MODES, GROUPS, 2, QUAD)
    out = np.zeros((GROUPS, 2, MODES, 2, GROUPS, 2, 2, QUAD), dtype=np.float32)
    for y in range(GROUPS):
        for slot in range(GROUPS):
            for part in range(2):
                out[y, part, :, :, slot, :, part, :] = v0[:, None, (y - slot) % GROUPS]
    return out.reshape(GROUPS, 2, MODES, 128)


def spectra_call(snapshots, half, tile):
    blocks_dev, window_len, rows_dev = snapshots.shape
    rows = OWNED * 2 * QUAD
    depth = QUAD * window_len
    part = rows_dev // HALVES
    steps = part // tile
    lhs_all = jnp.asarray(spectral_lhs())

    def kernel(lhs_ref, x_ref, *rest):
        outs, lhs = rest[:-1], rest[-1]

        @pl.when(pl.program_id(0) == 0)
        def _():
            for slot in range(GROUPS):
                owner = lax.rem(lax.axis_index("blk") + slot, GROUPS)
                lhs[slot * rows : (slot + 1) * rows, :] = lhs_ref[owner]

        data = x_ref[...].reshape(2, depth, tile)
        result = [jnp.dot(lhs[...], data[q], preferred_element_type=F32) for q in range(2)]
        for n, out in enumerate(outs):
            out[...] = jnp.concatenate(
                [
                    result[q][8 * m : 8 * m + 8]
                    for m in range(PAIR * n, PAIR * n + PAIR)
                    for q in range(2)
                ],
                axis=0,
            ).astype(BF16)

    out = pl.pallas_call(
        kernel,
        grid=(steps,),
        in_specs=[
            pl.BlockSpec((GROUPS, rows, depth), lambda n: (0, 0, 0)),
            pl.BlockSpec((blocks_dev, window_len, tile), lambda n: (0, 0, n + half * steps)),
        ],
        out_specs=[pl.BlockSpec((32, tile), lambda n: (0, n))] * (GROUPS * PAIR),
        scratch_shapes=[pltpu.VMEM((GROUPS * rows, depth), BF16)],
        out_shape=[jax.ShapeDtypeStruct((32, part), BF16)] * (GROUPS * PAIR),
        compiler_params=pltpu.CompilerParams(vmem_limit_bytes=LARGE),
        cost_estimate=pl.CostEstimate(
            flops=4 * GROUPS * rows * depth * part,
            bytes_accessed=4 * (depth + GROUPS * rows) * part,
            transcendentals=0,
        ),
        name="spectra",
    )(lhs_all, snapshots)
    return [[out[slot * PAIR + i] for slot in range(GROUPS)] for i in range(PAIR)]


def odd_lanes(shape):
    return (lax.broadcasted_iota(jnp.int32, shape, len(shape) - 1) & QUAD) == QUAD


def low_lanes(shape):
    return lax.broadcasted_iota(jnp.int32, shape, len(shape) - 1) < 64


def low_rows(shape):
    return lax.broadcasted_iota(jnp.int32, shape, len(shape) - 2) % 8 < QUAD


def other_lanes(value):
    axis = value.ndim - 1
    return jnp.where(
        odd_lanes(value.shape), pltpu.roll(value, QUAD, axis), pltpu.roll(value, 128 - QUAD, axis)
    )


def other_rows(value):
    rows = value.shape[0]
    return pltpu.roll(value.reshape(rows // 8, 8, 128), QUAD, 1).reshape(rows, 128)


def turned(value):
    other = other_lanes(value)
    return jnp.where(odd_lanes(value.shape), other, -other)


def gram_call(half, pieces, weights, pivot_local, before):
    part = pieces[0].shape[1]

    def kernel(p_ref, w_ref, *rest):
        x_refs, rest = rest[:GROUPS], rest[GROUPS:]
        out_ref = rest[-1]
        lane = lax.broadcasted_iota(jnp.int32, (MODES, part), 1) + half * part
        parts = []
        pivots = []
        for f in range(PAIR):
            x = jnp.concatenate([r[16 * f : 16 * f + 16] for r in x_refs], axis=0)
            wx = x.astype(F32) * w_ref[:, half * part : (half + 1) * part]
            hot = jnp.where(lane == p_ref[f], 1.0, 0.0)
            left = jnp.concatenate([wx, hot, jnp.zeros_like(hot)], axis=0).astype(BF16)
            total = lax.dot_general(left, x, (((1,), (1,)), ((), ())), preferred_element_type=F32)
            total = jnp.concatenate([total, total], axis=1)
            gram = total[:64]
            same = low_rows(gram.shape) != odd_lanes(gram.shape)
            cross = other_lanes(other_rows(gram)) + jnp.where(same, gram, -gram)
            cross = jnp.where(low_rows((32, 128)), cross[:32], other_rows(cross[32:]))
            packed = jnp.where(low_lanes((16, 128)), cross[:16], cross[16:])
            parts.append(packed)
            pivots.append(total[64:72])
        parts.append(jnp.where(low_lanes((MODES, 128)), pivots[0], pivots[1]))
        result = jnp.concatenate(parts, axis=0)
        out_ref[...] = result if before is None else result + rest[0][...]

    return pl.pallas_call(
        kernel,
        out_shape=jax.ShapeDtypeStruct((16 * PAIR + MODES, 128), F32),
        compiler_params=pltpu.CompilerParams(vmem_limit_bytes=SMALL),
        cost_estimate=pl.CostEstimate(
            flops=2 * PAIR * 64 * 256 * part, bytes_accessed=4 * 64 * part, transcendentals=0
        ),
        name="gram",
    )(pivot_local, weights, *pieces, *([] if before is None else [before]))


def split3(value):
    high = value.astype(BF16)
    rest = value - high.astype(F32)
    mid = rest.astype(BF16)
    low = (rest - mid.astype(F32)).astype(BF16)
    return high, mid, low


def right_side(cross):
    turn = turned(cross)
    first = low_rows(cross.shape)
    full = jnp.concatenate(
        [
            jnp.where(first, cross, other_rows(turn)),
            jnp.where(first, other_rows(cross), turn),
        ],
        axis=0,
    )
    full = jnp.concatenate([full, turned(full)], axis=1)
    high, mid, low = split3(full)
    return jnp.concatenate([high, mid, high, mid, low, high], axis=0)


def leading_basis(crosses, begin):
    count = len(crosses)
    rights = [right_side(cross) for cross in crosses]
    vec = jnp.stack([begin[0]] * count)
    alt = jnp.stack([begin[1]] * count)
    low_lane = low_lanes((MODES, 128))
    row = lax.broadcasted_iota(jnp.int32, (count, MODES, 1), 1)
    for _ in range(ITERS):
        new = []
        for f in range(count):
            high, mid, low = split3(vec[f])
            mixed = jnp.where(low_lane, high.astype(F32), low.astype(F32)).astype(BF16)
            left = jnp.concatenate([high, mid, mixed], axis=1)
            new.append(jnp.dot(left, rights[f], preferred_element_type=F32))
        new = jnp.stack(new)
        vec, alt = new[:, :, :128], new[:, :, 128:]
        scale = jnp.ones((count, MODES, 1), F32)
        for j in range(MODES):
            q = jnp.broadcast_to(vec[:, j : j + 1], vec.shape)
            q_alt = jnp.broadcast_to(alt[:, j : j + 1], vec.shape)
            power = jnp.sum(q * q, axis=2, keepdims=True)
            scale = jnp.where(row == j, lax.rsqrt(power * 0.5 + 1e-06), scale)
            if j < MODES - 1:
                inverse = jnp.where(row > j, 1.0 / (power + 2e-06), 0.0)
                coef_re = jnp.sum(vec * q, axis=2, keepdims=True) * inverse
                coef_im = jnp.sum(vec * q_alt, axis=2, keepdims=True) * inverse
                vec, alt = (
                    vec - (coef_re * q + coef_im * q_alt),
                    alt - (coef_re * q_alt - coef_im * q),
                )
        vec = vec * scale
        alt = alt * scale
    return vec, alt


def modes_call(pair, place, start, weights, degrees, sums, early, late, before, row_count):
    rows_dev = weights.shape[1]
    tile = rows_dev // HALVES
    bands = tile * DEGREES // row_count

    def kernel(place_ref, start_ref, w_ref, deg_ref, sum_ref, *rest):
        x_refs, rest = rest[: HALVES * GROUPS], rest[HALVES * GROUPS :]
        modes_ref, energy_ref, stage, sems = rest[-4:]
        total = jnp.sum(sum_ref[...], axis=0)
        crosses = []
        for f in range(PAIR):
            packed = total[16 * f : 16 * f + 16] * (1.0 / row_count)
            swap = pltpu.roll(packed, 64, 1)
            low = low_lanes(packed.shape)
            crosses.append(
                jnp.concatenate(
                    [jnp.where(low, packed, swap), jnp.where(low, swap, packed)], axis=0
                )
            )
        vec, alt = leading_basis(crosses, start_ref[place_ref[0]])
        odd = odd_lanes(vec.shape)
        low = low_lanes(vec.shape)
        upper = jnp.where(odd, -vec, vec).astype(BF16).astype(F32)
        lower = jnp.where(odd, alt, -alt).astype(BF16).astype(F32)
        pivots = total[16 * PAIR :]
        at = jnp.where(low, jnp.stack([pivots, pltpu.roll(pivots, 64, 1)]), 0.0)
        z_re = jnp.sum(upper * at, axis=2, keepdims=True)
        z_im = jnp.sum(lower * at, axis=2, keepdims=True)
        inverse = lax.rsqrt(z_re * z_re + z_im * z_im + 1.0)
        s_re = z_re * inverse
        s_im = z_im * inverse
        expand = jnp.concatenate([upper, lower], axis=1).astype(BF16)
        total = jnp.zeros((MODES, 128), F32) if before is None else rest[1][...]

        lane = lax.broadcasted_iota(jnp.int32, (MODES, 128), 1)
        copies = []
        for half in range(HALVES):
            span = slice(half * tile, (half + 1) * tile)
            w = w_ref[:, span]
            level_of = deg_ref[:, span]
            base = place_ref[1] + half * bands
            hits = [level_of == base + m for m in range(bands + 1)]
            for f in range(PAIR):
                rows = slice(16 * f, 16 * f + 16)
                x = jnp.concatenate(
                    [r[rows] for r in x_refs[GROUPS * half : GROUPS * half + GROUPS]], axis=0
                )
                psi = jnp.dot(expand[f][:, :64], x, preferred_element_type=F32)
                p_re, p_im = psi[:8], psi[8:]
                out_re = p_re * s_re[f] + p_im * s_im[f]
                out_im = p_im * s_re[f] - p_re * s_im[f]
                stage[half, f, 0] = out_re.astype(BF16)
                stage[half, f, 1] = out_im.astype(BF16)
                power = w * (out_re * out_re + out_im * out_im)
                for m in range(bands + 1):
                    level = jnp.sum(jnp.where(hits[m], power, 0.0), axis=1, keepdims=True)
                    spot = (pair * PAIR + f) * 32 + place_ref[2] + half * bands + m
                    total = total + jnp.where(lane == spot, level * (DEGREES / row_count), 0.0)
            copy = pltpu.make_async_copy(
                stage.at[half],
                modes_ref.at[pl.ds(pair * PAIR, PAIR), :, :, pl.ds(half * tile, tile)],
                sems.at[half],
            )
            copy.start()
            copies.append(copy)
        energy_ref[...] = total
        for copy in copies:
            copy.wait()

    vmem = pl.BlockSpec(memory_space=pltpu.VMEM)
    raw = pl.BlockSpec(memory_space=pl.ANY)
    args = [place, start, weights, degrees, sums, *early, *late]
    in_specs = [pl.BlockSpec(memory_space=pltpu.SMEM)] + [vmem] * (len(args) - 1)
    aliases = {}
    if before is not None:
        in_specs += [raw, vmem]
        aliases = {len(args): 0}
        args += list(before)
    return pl.pallas_call(
        kernel,
        in_specs=in_specs,
        out_specs=[raw, vmem],
        scratch_shapes=[
            pltpu.VMEM((HALVES, PAIR, 2, MODES, tile), BF16),
            pltpu.SemaphoreType.DMA((HALVES,)),
        ],
        out_shape=[
            jax.ShapeDtypeStruct((OWNED, 2, MODES, rows_dev), BF16),
            jax.ShapeDtypeStruct((MODES, 128), F32),
        ],
        input_output_aliases=aliases,
        compiler_params=pltpu.CompilerParams(vmem_limit_bytes=SMALL),
        cost_estimate=pl.CostEstimate(
            flops=2 * PAIR * 64 * 256 * rows_dev + 10**9,
            bytes_accessed=PAIR * 2 * 80 * rows_dev,
            transcendentals=0,
        ),
        name="modes",
    )(*args)


def energy_call(gathered):
    chips = gathered.shape[0]

    def kernel(in_ref, out_ref):
        out_ref[...] = jnp.zeros_like(out_ref)
        lane = lax.broadcasted_iota(jnp.int32, (MODES, 128), 1)
        for c in range(chips):
            value = in_ref[c]
            for f in range(OWNED):
                begin = c * 2 * LEVELS
                piece = jnp.where((lane >= 32 * f) & (lane < 32 * f + 2 * LEVELS + 1), value, 0.0)
                shift = (begin - 32 * f) % 128
                piece = pltpu.roll(piece, shift, 1) if shift else piece
                column = begin // 128
                split = 128 - begin % 128
                if split >= 2 * LEVELS + 1:
                    out_ref[f, :, column * 128 : column * 128 + 128] += piece
                else:
                    head = jnp.where(lane >= begin % 128, piece, 0.0)
                    out_ref[f, :, column * 128 : column * 128 + 128] += head
                    if (column + 1) * 128 < DEGREES:
                        out_ref[f, :, (column + 1) * 128 : (column + 2) * 128] += piece - head

    return pl.pallas_call(
        kernel,
        out_shape=jax.ShapeDtypeStruct((OWNED, MODES, DEGREES), F32),
        name="energy",
    )(gathered)


def gather_chips(value):
    value = value + lax.ppermute(value, "core", [(0, 1), (1, 0)])
    chips = STATE[0] * STATE[1]
    spread = jnp.broadcast_to(value[None], (chips,) + value.shape)
    return lax.all_to_all(spread, ("z", "x"), 0, 0, tiled=True)


def after(value, first):
    return lax.optimization_barrier((value, first))[0]


def per_device(snapshots, weights, degrees, pivots):
    rows_dev = snapshots.shape[2]
    row_count = rows_dev * DEVICES
    core = lax.axis_index("core").astype(jnp.int32)
    state = (lax.axis_index(("z", "x", "core"))).astype(jnp.int32)
    y = lax.axis_index("blk").astype(jnp.int32)
    place = jnp.stack([y, state * LEVELS, core * LEVELS])
    pivot_local = (pivots - state * rows_dev)[:, :, None]
    weights = weights.reshape(1, rows_dev)
    degrees = degrees.reshape(1, rows_dev)
    start = jnp.asarray(start_basis())

    halves = [spectra_call(snapshots, half, 4096) for half in range(HALVES)]
    pieces = {}
    for pair in range(PAIR):
        for half in range(HALVES):
            sent = halves[half][pair]
            pieces[pair, half] = [sent[0]] + [
                lax.ppermute(sent[k], "blk", [(g, (g + k) % GROUPS) for g in range(GROUPS)])
                for k in range(1, GROUPS)
            ]
    before = None
    for pair in range(PAIR):
        gram = None
        for half in range(HALVES):
            known = weights if before is None or half < HALVES - 1 else after(weights, before[1])
            gram = gram_call(
                half, pieces[pair, half], known, pivot_local[PAIR * pair : PAIR * pair + PAIR], gram
            )
        before = modes_call(
            pair, place, start, weights, degrees, gather_chips(gram),
            pieces[pair, 0], pieces[pair, 1], before, row_count,
        )
    modes, energy = before
    return modes, energy_call(gather_chips(energy))


def solution(mesh):
    fine = Mesh(mesh.devices.reshape(*STATE, GROUPS), ("z", "x", "core", "blk"))
    state = ("z", "x", "core")
    return jax.shard_map(
        per_device,
        mesh=fine,
        in_specs=(P("blk", None, state), P(state), P(state), P("blk", None)),
        out_specs=(P("blk", None, None, state), P("blk", None, None)),
        check_vma=False,
    )
```

```python
import functools
import math

import jax
import jax.numpy as jnp
import numpy as np
from jax import lax
from jax.experimental import pallas as pl
from jax.experimental.pallas import tpu as pltpu
from jax.sharding import Mesh
from jax.sharding import PartitionSpec as P

NF = 16
DEGREES = 384
ITERS = 6
MODES = 8
WINDOW = 64
GROUPS = 4
PER_GROUP = 8
QUAD = 4
OWNED = 4
PAIR = 2
HALVES = 2
BLOCKS = GROUPS * PER_GROUP
STATE = (4, 4, 2)
DEVICES = 32
LEVELS = DEGREES // DEVICES
F32 = jnp.float32
BF16 = jnp.bfloat16
LARGE = 60 * 1024 * 1024
SMALL = 24 * 1024 * 1024


def dft_table():
    t = np.arange(WINDOW, dtype=np.int32)
    order = np.arange(1, NF + 1, dtype=np.int32)
    two_pi = np.float32(2.0 * math.pi)
    window = np.float32(0.5) - np.float32(0.5) * np.cos(two_pi * t.astype(np.float32) / np.float32(WINDOW))
    norm = np.sqrt(np.sum(window * window))
    turns = order[:, None] * t[None, :] % WINDOW
    angle = two_pi * turns.astype(np.float32) / np.float32(WINDOW)
    table = np.stack([window * np.cos(angle) / norm, -window * np.sin(angle) / norm], axis=1)
    return table.astype(BF16)


def spectral_lhs():
    table = dft_table()
    lhs = np.zeros((GROUPS, OWNED, 2, QUAD, QUAD, WINDOW), dtype=BF16)
    for owner in range(GROUPS):
        for i in range(OWNED):
            for b in range(QUAD):
                lhs[owner, i, :, b, b, :] = table[OWNED * owner + i]
    return lhs.reshape(GROUPS, OWNED * 2 * QUAD, QUAD * WINDOW)


def start_basis():
    b = np.arange(BLOCKS, dtype=np.float32)
    j = np.arange(MODES, dtype=np.float32)
    v0 = np.cos(np.float32(math.pi) * (j[:, None] + np.float32(0.5)) * (b[None, :] + np.float32(0.5)) / np.float32(BLOCKS))
    v0 = (v0 * np.float32(math.sqrt(2.0 / BLOCKS))).reshape(MODES, GROUPS, 2, QUAD)
    out = np.zeros((GROUPS, 2, MODES, 2, GROUPS, 2, 2, QUAD), dtype=np.float32)
    for y in range(GROUPS):
        for slot in range(GROUPS):
            for part in range(2):
                out[y, part, :, :, slot, :, part, :] = v0[:, None, (y - slot) % GROUPS]
    return out.reshape(GROUPS, 2, MODES, 128)


def spectra_call(snapshots, half, tile):
    blocks_dev, window_len, rows_dev = snapshots.shape
    rows = OWNED * 2 * QUAD
    depth = QUAD * window_len
    part = rows_dev // HALVES
    steps = part // tile
    lhs_all = jnp.asarray(spectral_lhs())

    def kernel(lhs_ref, x_ref, *rest):
        outs, lhs = rest[:-1], rest[-1]

        @pl.when(pl.program_id(0) == 0)
        def _():
            for slot in range(GROUPS):
                owner = lax.rem(lax.axis_index("blk") + slot, GROUPS)
                lhs[slot * rows : (slot + 1) * rows, :] = lhs_ref[owner]

        data = x_ref[...].reshape(2, depth, tile)
        result = [jnp.dot(lhs[...], data[q], preferred_element_type=F32) for q in range(2)]
        for n, out in enumerate(outs):
            out[...] = jnp.concatenate(
                [
                    result[q][8 * m : 8 * m + 8]
                    for m in range(PAIR * n, PAIR * n + PAIR)
                    for q in range(2)
                ],
                axis=0,
            ).astype(BF16)

    out = pl.pallas_call(
        kernel,
        grid=(steps,),
        in_specs=[
            pl.BlockSpec((GROUPS, rows, depth), lambda n: (0, 0, 0)),
            pl.BlockSpec((blocks_dev, window_len, tile), lambda n: (0, 0, n + half * steps)),
        ],
        out_specs=[pl.BlockSpec((32, tile), lambda n: (0, n))] * (GROUPS * PAIR),
        scratch_shapes=[pltpu.VMEM((GROUPS * rows, depth), BF16)],
        out_shape=[jax.ShapeDtypeStruct((32, part), BF16)] * (GROUPS * PAIR),
        compiler_params=pltpu.CompilerParams(vmem_limit_bytes=LARGE),
        cost_estimate=pl.CostEstimate(
            flops=4 * GROUPS * rows * depth * part,
            bytes_accessed=4 * (depth + GROUPS * rows) * part,
            transcendentals=0,
        ),
        name="spectra",
    )(lhs_all, snapshots)
    return [[out[slot * PAIR + i] for slot in range(GROUPS)] for i in range(PAIR)]


def odd_lanes(shape):
    return (lax.broadcasted_iota(jnp.int32, shape, len(shape) - 1) & QUAD) == QUAD


def low_lanes(shape):
    return lax.broadcasted_iota(jnp.int32, shape, len(shape) - 1) < 64


def low_rows(shape):
    return lax.broadcasted_iota(jnp.int32, shape, len(shape) - 2) % 8 < QUAD


def other_lanes(value):
    axis = value.ndim - 1
    return jnp.where(
        odd_lanes(value.shape), pltpu.roll(value, QUAD, axis), pltpu.roll(value, 128 - QUAD, axis)
    )


def other_rows(value):
    rows = value.shape[0]
    return pltpu.roll(value.reshape(rows // 8, 8, 128), QUAD, 1).reshape(rows, 128)


def turned(value):
    other = other_lanes(value)
    return jnp.where(odd_lanes(value.shape), other, -other)


def gram_call(half, pieces, weights, pivot_local, before):
    part = pieces[0].shape[1]

    def kernel(p_ref, w_ref, *rest):
        x_refs, rest = rest[:GROUPS], rest[GROUPS:]
        out_ref = rest[-1]
        lane = lax.broadcasted_iota(jnp.int32, (MODES, part), 1) + half * part
        for f in range(PAIR):
            x = jnp.concatenate([r[16 * f : 16 * f + 16] for r in x_refs], axis=0)
            wx = x.astype(F32) * w_ref[:, half * part : (half + 1) * part]
            hot = jnp.where(lane == p_ref[f], 1.0, 0.0)
            left = jnp.concatenate([wx, hot, jnp.zeros_like(hot)], axis=0).astype(BF16)
            total = lax.dot_general(left, x, (((1,), (1,)), ((), ())), preferred_element_type=F32)
            total = jnp.concatenate([total, total], axis=1)
            gram = total[:64]
            same = low_rows(gram.shape) != odd_lanes(gram.shape)
            cross = other_lanes(other_rows(gram)) + jnp.where(same, gram, -gram)
            cross = jnp.where(low_rows((32, 128)), cross[:32], other_rows(cross[32:]))
            packed = jnp.where(low_lanes((16, 128)), cross[:16], cross[16:])
            packed = jnp.concatenate([packed, total[64:72]], axis=0)
            if before is not None:
                packed = packed + rest[0][f]
            out_ref[f] = packed

    return pl.pallas_call(
        kernel,
        out_shape=jax.ShapeDtypeStruct((PAIR, 24, 128), F32),
        compiler_params=pltpu.CompilerParams(vmem_limit_bytes=SMALL),
        cost_estimate=pl.CostEstimate(
            flops=2 * PAIR * 64 * 256 * part, bytes_accessed=4 * 64 * part, transcendentals=0
        ),
        name="gram",
    )(pivot_local, weights, *pieces, *([] if before is None else [before]))


def split3(value):
    high = value.astype(BF16)
    rest = value - high.astype(F32)
    mid = rest.astype(BF16)
    low = (rest - mid.astype(F32)).astype(BF16)
    return high, mid, low


def right_side(cross):
    turn = turned(cross)
    first = low_rows(cross.shape)
    full = jnp.concatenate(
        [
            jnp.where(first, cross, other_rows(turn)),
            jnp.where(first, other_rows(cross), turn),
        ],
        axis=0,
    )
    full = jnp.concatenate([full, turned(full)], axis=1)
    high, mid, low = split3(full)
    return jnp.concatenate([high, mid, high, mid, low, high], axis=0)


def leading_basis(crosses, begin):
    count = len(crosses)
    rights = [right_side(cross) for cross in crosses]
    vec = jnp.stack([begin[0]] * count)
    alt = jnp.stack([begin[1]] * count)
    low_lane = low_lanes((MODES, 128))
    row = lax.broadcasted_iota(jnp.int32, (count, MODES, 1), 1)
    for _ in range(ITERS):
        new = []
        for f in range(count):
            high, mid, low = split3(vec[f])
            mixed = jnp.where(low_lane, high.astype(F32), low.astype(F32)).astype(BF16)
            left = jnp.concatenate([high, mid, mixed], axis=1)
            new.append(jnp.dot(left, rights[f], preferred_element_type=F32))
        new = jnp.stack(new)
        vec, alt = new[:, :, :128], new[:, :, 128:]
        scale = jnp.ones((count, MODES, 1), F32)
        for j in range(MODES):
            q = jnp.broadcast_to(vec[:, j : j + 1], vec.shape)
            q_alt = jnp.broadcast_to(alt[:, j : j + 1], vec.shape)
            power = jnp.sum(q * q, axis=2, keepdims=True)
            scale = jnp.where(row == j, lax.rsqrt(power * 0.5 + 1e-06), scale)
            if j < MODES - 1:
                inverse = jnp.where(row > j, 1.0 / (power + 2e-06), 0.0)
                coef_re = jnp.sum(vec * q, axis=2, keepdims=True) * inverse
                coef_im = jnp.sum(vec * q_alt, axis=2, keepdims=True) * inverse
                vec, alt = (
                    vec - (coef_re * q + coef_im * q_alt),
                    alt - (coef_re * q_alt - coef_im * q),
                )
        vec = vec * scale
        alt = alt * scale
    return vec, alt


def modes_call(pair, place, start, weights, degrees, sums, early, late, before, row_count):
    rows_dev = weights.shape[1]
    tile = rows_dev // HALVES
    bands = tile * DEGREES // row_count

    def kernel(place_ref, start_ref, w_ref, deg_ref, sum_ref, *rest):
        x_refs, rest = rest[: HALVES * GROUPS], rest[HALVES * GROUPS :]
        modes_ref, energy_ref, stage, held, sems, x_sems = rest[-6:]
        fetches = []
        for i, r in enumerate(x_refs):
            fetch = pltpu.make_async_copy(r, held.at[i], x_sems.at[i])
            fetch.start()
            fetches.append(fetch)
        total = jnp.sum(sum_ref[...], axis=0)
        crosses = []
        for f in range(PAIR):
            packed = total[f, :16] * (1.0 / row_count)
            swap = pltpu.roll(packed, 64, 1)
            low = low_lanes(packed.shape)
            crosses.append(
                jnp.concatenate(
                    [jnp.where(low, packed, swap), jnp.where(low, swap, packed)], axis=0
                )
            )
        vec, alt = leading_basis(crosses, start_ref[place_ref[0]])
        odd = odd_lanes(vec.shape)
        low = low_lanes(vec.shape)
        upper = jnp.where(odd, -vec, vec).astype(BF16).astype(F32)
        lower = jnp.where(odd, alt, -alt).astype(BF16).astype(F32)
        at = jnp.where(low, total[:, 16:24], 0.0)
        z_re = jnp.sum(upper * at, axis=2, keepdims=True)
        z_im = jnp.sum(lower * at, axis=2, keepdims=True)
        inverse = lax.rsqrt(z_re * z_re + z_im * z_im + 1.0)
        s_re = z_re * inverse
        s_im = z_im * inverse
        expand = jnp.concatenate([upper, lower], axis=1).astype(BF16)
        total = jnp.zeros((MODES, 128), F32) if before is None else rest[1][...]

        lane = lax.broadcasted_iota(jnp.int32, (MODES, 128), 1)
        copies = []
        for half in range(HALVES):
            for fetch in fetches[GROUPS * half : GROUPS * half + GROUPS]:
                fetch.wait()
            span = slice(half * tile, (half + 1) * tile)
            w = w_ref[:, span]
            level_of = deg_ref[:, span]
            base = place_ref[1] + half * bands
            hits = [level_of == base + m for m in range(bands + 1)]
            for f in range(PAIR):
                rows = slice(16 * f, 16 * f + 16)
                x = jnp.concatenate(
                    [held[GROUPS * half + k, rows] for k in range(GROUPS)], axis=0
                )
                psi = jnp.dot(expand[f][:, :64], x, preferred_element_type=F32)
                p_re, p_im = psi[:8], psi[8:]
                out_re = p_re * s_re[f] + p_im * s_im[f]
                out_im = p_im * s_re[f] - p_re * s_im[f]
                stage[half, f, 0] = out_re.astype(BF16)
                stage[half, f, 1] = out_im.astype(BF16)
                power = w * (out_re * out_re + out_im * out_im)
                for m in range(bands + 1):
                    level = jnp.sum(jnp.where(hits[m], power, 0.0), axis=1, keepdims=True)
                    spot = (pair * PAIR + f) * 32 + place_ref[2] + half * bands + m
                    total = total + jnp.where(lane == spot, level * (DEGREES / row_count), 0.0)
            copy = pltpu.make_async_copy(
                stage.at[half],
                modes_ref.at[pl.ds(pair * PAIR, PAIR), :, :, pl.ds(half * tile, tile)],
                sems.at[half],
            )
            copy.start()
            copies.append(copy)
        energy_ref[...] = total
        for copy in copies:
            copy.wait()

    vmem = pl.BlockSpec(memory_space=pltpu.VMEM)
    raw = pl.BlockSpec(memory_space=pl.ANY)
    args = [place, start, weights, degrees, sums, *early, *late]
    source = pl.BlockSpec(memory_space=pltpu.HBM)
    in_specs = [pl.BlockSpec(memory_space=pltpu.SMEM)] + [vmem] * 4 + [source] * (HALVES * GROUPS)
    aliases = {}
    if before is not None:
        in_specs += [raw, vmem]
        aliases = {len(args): 0}
        args += list(before)
    return pl.pallas_call(
        kernel,
        in_specs=in_specs,
        out_specs=[raw, vmem],
        scratch_shapes=[
            pltpu.VMEM((HALVES, PAIR, 2, MODES, tile), BF16),
            pltpu.VMEM((HALVES * GROUPS, 16 * PAIR, tile), BF16),
            pltpu.SemaphoreType.DMA((HALVES,)),
            pltpu.SemaphoreType.DMA((HALVES * GROUPS,)),
        ],
        out_shape=[
            jax.ShapeDtypeStruct((OWNED, 2, MODES, rows_dev), BF16),
            jax.ShapeDtypeStruct((MODES, 128), F32),
        ],
        input_output_aliases=aliases,
        compiler_params=pltpu.CompilerParams(vmem_limit_bytes=SMALL),
        cost_estimate=pl.CostEstimate(
            flops=2 * PAIR * 64 * 256 * rows_dev + 10**9,
            bytes_accessed=PAIR * 2 * 80 * rows_dev,
            transcendentals=0,
        ),
        name="modes",
    )(*args)


def energy_call(gathered):
    chips = gathered.shape[0]

    def kernel(in_ref, out_ref):
        out_ref[...] = jnp.zeros_like(out_ref)
        lane = lax.broadcasted_iota(jnp.int32, (MODES, 128), 1)
        for c in range(chips):
            value = in_ref[c]
            for f in range(OWNED):
                begin = c * 2 * LEVELS
                piece = jnp.where((lane >= 32 * f) & (lane < 32 * f + 2 * LEVELS + 1), value, 0.0)
                shift = (begin - 32 * f) % 128
                piece = pltpu.roll(piece, shift, 1) if shift else piece
                column = begin // 128
                split = 128 - begin % 128
                if split >= 2 * LEVELS + 1:
                    out_ref[f, :, column * 128 : column * 128 + 128] += piece
                else:
                    head = jnp.where(lane >= begin % 128, piece, 0.0)
                    out_ref[f, :, column * 128 : column * 128 + 128] += head
                    if (column + 1) * 128 < DEGREES:
                        out_ref[f, :, (column + 1) * 128 : (column + 2) * 128] += piece - head

    return pl.pallas_call(
        kernel,
        out_shape=jax.ShapeDtypeStruct((OWNED, MODES, DEGREES), F32),
        name="energy",
    )(gathered)


def gather_chips(value):
    value = value + lax.ppermute(value, "core", [(0, 1), (1, 0)])
    chips = STATE[0] * STATE[1]
    spread = jnp.broadcast_to(value[None], (chips,) + value.shape)
    return lax.all_to_all(spread, ("z", "x"), 0, 0, tiled=True)


def after(value, first):
    return lax.optimization_barrier((value, first))[0]


def per_device(snapshots, weights, degrees, pivots):
    rows_dev = snapshots.shape[2]
    row_count = rows_dev * DEVICES
    core = lax.axis_index("core").astype(jnp.int32)
    state = (lax.axis_index(("z", "x", "core"))).astype(jnp.int32)
    y = lax.axis_index("blk").astype(jnp.int32)
    place = jnp.stack([y, state * LEVELS, core * LEVELS])
    pivot_local = (pivots - state * rows_dev)[:, :, None]
    weights = weights.reshape(1, rows_dev)
    degrees = degrees.reshape(1, rows_dev)
    start = jnp.asarray(start_basis())

    halves = [spectra_call(snapshots, half, 4096) for half in range(HALVES)]
    pieces = {}
    for pair in range(PAIR):
        for half in range(HALVES):
            sent = halves[half][pair]
            pieces[pair, half] = [sent[0]] + [
                lax.ppermute(sent[k], "blk", [(g, (g + k) % GROUPS) for g in range(GROUPS)])
                for k in range(1, GROUPS)
            ]
    before = None
    for pair in range(PAIR):
        gram = None
        for half in range(HALVES):
            known = weights if before is None or half < HALVES - 1 else after(weights, before[1])
            gram = gram_call(
                half, pieces[pair, half], known, pivot_local[PAIR * pair : PAIR * pair + PAIR], gram
            )
        before = modes_call(
            pair, place, start, weights, degrees, gather_chips(gram),
            pieces[pair, 0], pieces[pair, 1], before, row_count,
        )
    modes, energy = before
    return modes, energy_call(gather_chips(energy))


def solution(mesh):
    fine = Mesh(mesh.devices.reshape(*STATE, GROUPS), ("z", "x", "core", "blk"))
    state = ("z", "x", "core")
    return jax.shard_map(
        per_device,
        mesh=fine,
        in_specs=(P("blk", None, state), P(state), P(state), P("blk", None)),
        out_specs=(P("blk", None, None, state), P("blk", None, None)),
        check_vma=False,
    )
```

```python
import functools
import math

import jax
import jax.numpy as jnp
import numpy as np
from jax import lax
from jax.experimental import pallas as pl
from jax.experimental.pallas import tpu as pltpu
from jax.sharding import Mesh
from jax.sharding import PartitionSpec as P

NF = 16
DEGREES = 384
ITERS = 6
MODES = 8
WINDOW = 64
GROUPS = 4
PER_GROUP = 8
QUAD = 4
OWNED = 4
PAIR = 2
HALVES = 2
BLOCKS = GROUPS * PER_GROUP
STATE = (4, 4, 2)
DEVICES = 32
LEVELS = DEGREES // DEVICES
F32 = jnp.float32
BF16 = jnp.bfloat16
LARGE = 60 * 1024 * 1024
SMALL = 24 * 1024 * 1024


def dft_table():
    t = np.arange(WINDOW, dtype=np.int32)
    order = np.arange(1, NF + 1, dtype=np.int32)
    two_pi = np.float32(2.0 * math.pi)
    window = np.float32(0.5) - np.float32(0.5) * np.cos(two_pi * t.astype(np.float32) / np.float32(WINDOW))
    norm = np.sqrt(np.sum(window * window))
    turns = order[:, None] * t[None, :] % WINDOW
    angle = two_pi * turns.astype(np.float32) / np.float32(WINDOW)
    table = np.stack([window * np.cos(angle) / norm, -window * np.sin(angle) / norm], axis=1)
    return table.astype(BF16)


def spectral_lhs():
    table = dft_table()
    lhs = np.zeros((GROUPS, OWNED, 2, QUAD, QUAD, WINDOW), dtype=BF16)
    for owner in range(GROUPS):
        for i in range(OWNED):
            for b in range(QUAD):
                lhs[owner, i, :, b, b, :] = table[OWNED * owner + i]
    return lhs.reshape(GROUPS, OWNED * 2 * QUAD, QUAD * WINDOW)


def start_basis():
    b = np.arange(BLOCKS, dtype=np.float32)
    j = np.arange(MODES, dtype=np.float32)
    v0 = np.cos(np.float32(math.pi) * (j[:, None] + np.float32(0.5)) * (b[None, :] + np.float32(0.5)) / np.float32(BLOCKS))
    v0 = (v0 * np.float32(math.sqrt(2.0 / BLOCKS))).reshape(MODES, GROUPS, 2, QUAD)
    out = np.zeros((GROUPS, 2, MODES, 2, GROUPS, 2, 2, QUAD), dtype=np.float32)
    for y in range(GROUPS):
        for slot in range(GROUPS):
            for part in range(2):
                out[y, part, :, :, slot, :, part, :] = v0[:, None, (y - slot) % GROUPS]
    return out.reshape(GROUPS, 2, MODES, 128)


def spectra_call(snapshots, half, tile):
    blocks_dev, window_len, rows_dev = snapshots.shape
    rows = OWNED * 2 * QUAD
    depth = QUAD * window_len
    part = rows_dev // HALVES
    steps = part // tile
    lhs_all = jnp.asarray(spectral_lhs())

    def kernel(lhs_ref, x_ref, *rest):
        outs, lhs = rest[:-1], rest[-1]

        @pl.when(pl.program_id(0) == 0)
        def _():
            for slot in range(GROUPS):
                owner = lax.rem(lax.axis_index("blk") + slot, GROUPS)
                lhs[slot * rows : (slot + 1) * rows, :] = lhs_ref[owner]

        data = x_ref[...].reshape(2, depth, tile)
        result = [jnp.dot(lhs[...], data[q], preferred_element_type=F32) for q in range(2)]
        for n, out in enumerate(outs):
            out[...] = jnp.concatenate(
                [
                    result[q][8 * m : 8 * m + 8]
                    for m in range(PAIR * n, PAIR * n + PAIR)
                    for q in range(2)
                ],
                axis=0,
            ).astype(BF16)

    out = pl.pallas_call(
        kernel,
        grid=(steps,),
        in_specs=[
            pl.BlockSpec((GROUPS, rows, depth), lambda n: (0, 0, 0)),
            pl.BlockSpec((blocks_dev, window_len, tile), lambda n: (0, 0, n + half * steps)),
        ],
        out_specs=[pl.BlockSpec((32, tile), lambda n: (0, n))] * (GROUPS * PAIR),
        scratch_shapes=[pltpu.VMEM((GROUPS * rows, depth), BF16)],
        out_shape=[jax.ShapeDtypeStruct((32, part), BF16)] * (GROUPS * PAIR),
        compiler_params=pltpu.CompilerParams(vmem_limit_bytes=LARGE),
        cost_estimate=pl.CostEstimate(
            flops=4 * GROUPS * rows * depth * part,
            bytes_accessed=4 * (depth + GROUPS * rows) * part,
            transcendentals=0,
        ),
        name="spectra",
    )(lhs_all, snapshots)
    return [[out[slot * PAIR + i] for slot in range(GROUPS)] for i in range(PAIR)]


def odd_lanes(shape):
    return (lax.broadcasted_iota(jnp.int32, shape, len(shape) - 1) & QUAD) == QUAD


def low_lanes(shape):
    return lax.broadcasted_iota(jnp.int32, shape, len(shape) - 1) < 64


def low_rows(shape):
    return lax.broadcasted_iota(jnp.int32, shape, len(shape) - 2) % 8 < QUAD


def other_lanes(value):
    axis = value.ndim - 1
    return jnp.where(
        odd_lanes(value.shape), pltpu.roll(value, QUAD, axis), pltpu.roll(value, 128 - QUAD, axis)
    )


def other_rows(value):
    rows = value.shape[0]
    return pltpu.roll(value.reshape(rows // 8, 8, 128), QUAD, 1).reshape(rows, 128)


def turned(value):
    other = other_lanes(value)
    return jnp.where(odd_lanes(value.shape), other, -other)


def gram_call(half, pieces, weights, pivot_local, before, rows):
    part = pieces[0].shape[1]

    def kernel(p_ref, w_ref, *rest):
        x_refs, rest = rest[:GROUPS], rest[GROUPS:]
        out_ref = rest[-1]
        lane = lax.broadcasted_iota(jnp.int32, (MODES, part), 1) + half * part
        parts = []
        pivots = []
        for f in range(PAIR):
            x = jnp.concatenate([r[16 * f : 16 * f + 16] for r in x_refs], axis=0)
            wx = x.astype(F32) * w_ref[:, half * part : (half + 1) * part]
            hot = jnp.where(lane == p_ref[f], 1.0, 0.0)
            left = jnp.concatenate([wx, hot, jnp.zeros_like(hot)], axis=0).astype(BF16)
            total = lax.dot_general(left, x, (((1,), (1,)), ((), ())), preferred_element_type=F32)
            total = jnp.concatenate([total, total], axis=1)
            gram = total[:64]
            same = low_rows(gram.shape) != odd_lanes(gram.shape)
            cross = other_lanes(other_rows(gram)) + jnp.where(same, gram, -gram)
            cross = jnp.where(low_rows((32, 128)), cross[:32], other_rows(cross[32:]))
            packed = jnp.where(low_lanes((16, 128)), cross[:16], cross[16:])
            parts.append(packed)
            pivots.append(total[64:72])
        parts.append(jnp.where(low_lanes((MODES, 128)), pivots[0], pivots[1]))
        if rows > 16 * PAIR + MODES:
            parts.append(jnp.zeros((rows - 16 * PAIR - MODES, 128), F32))
        result = jnp.concatenate(parts, axis=0)
        out_ref[...] = result if before is None else result + rest[0][...]

    return pl.pallas_call(
        kernel,
        out_shape=jax.ShapeDtypeStruct((rows, 128), F32),
        compiler_params=pltpu.CompilerParams(vmem_limit_bytes=SMALL),
        cost_estimate=pl.CostEstimate(
            flops=2 * PAIR * 64 * 256 * part, bytes_accessed=4 * 64 * part, transcendentals=0
        ),
        name="gram",
    )(pivot_local, weights, *pieces, *([] if before is None else [before]))


def split3(value):
    high = value.astype(BF16)
    rest = value - high.astype(F32)
    mid = rest.astype(BF16)
    low = (rest - mid.astype(F32)).astype(BF16)
    return high, mid, low


def right_side(cross):
    turn = turned(cross)
    first = low_rows(cross.shape)
    full = jnp.concatenate(
        [
            jnp.where(first, cross, other_rows(turn)),
            jnp.where(first, other_rows(cross), turn),
        ],
        axis=0,
    )
    full = jnp.concatenate([full, turned(full)], axis=1)
    high, mid, low = split3(full)
    return jnp.concatenate([high, mid, high, mid, low, high], axis=0)


def leading_basis(crosses, begin):
    count = len(crosses)
    rights = [right_side(cross) for cross in crosses]
    vec = jnp.stack([begin[0]] * count)
    alt = jnp.stack([begin[1]] * count)
    low_lane = low_lanes((MODES, 128))
    row = lax.broadcasted_iota(jnp.int32, (count, MODES, 1), 1)
    for _ in range(ITERS):
        new = []
        for f in range(count):
            high, mid, low = split3(vec[f])
            mixed = jnp.where(low_lane, high.astype(F32), low.astype(F32)).astype(BF16)
            left = jnp.concatenate([high, mid, mixed], axis=1)
            new.append(jnp.dot(left, rights[f], preferred_element_type=F32))
        new = jnp.stack(new)
        vec, alt = new[:, :, :128], new[:, :, 128:]
        scale = jnp.ones((count, MODES, 1), F32)
        for j in range(MODES):
            q = jnp.broadcast_to(vec[:, j : j + 1], vec.shape)
            q_alt = jnp.broadcast_to(alt[:, j : j + 1], vec.shape)
            power = jnp.sum(q * q, axis=2, keepdims=True)
            scale = jnp.where(row == j, lax.rsqrt(power * 0.5 + 1e-06), scale)
            if j < MODES - 1:
                inverse = jnp.where(row > j, 1.0 / (power + 2e-06), 0.0)
                coef_re = jnp.sum(vec * q, axis=2, keepdims=True) * inverse
                coef_im = jnp.sum(vec * q_alt, axis=2, keepdims=True) * inverse
                vec, alt = (
                    vec - (coef_re * q + coef_im * q_alt),
                    alt - (coef_re * q_alt - coef_im * q),
                )
        vec = vec * scale
        alt = alt * scale
    return vec, alt


def modes_call(pair, place, start, weights, degrees, sums, early, late, before, row_count):
    rows_dev = weights.shape[1]
    tile = rows_dev // HALVES
    bands = tile * DEGREES // row_count

    def kernel(place_ref, start_ref, w_ref, deg_ref, sum_ref, *rest):
        x_refs, rest = rest[: HALVES * GROUPS], rest[HALVES * GROUPS :]
        modes_ref, energy_ref, stage, held, sems, x_sems = rest[-6:]
        fetches = []
        for i, r in enumerate(x_refs):
            fetch = pltpu.make_async_copy(r, held.at[i], x_sems.at[i])
            fetch.start()
            fetches.append(fetch)
        total = jnp.sum(sum_ref[...], axis=0)
        crosses = []
        for f in range(PAIR):
            packed = total[16 * f : 16 * f + 16] * (1.0 / row_count)
            swap = pltpu.roll(packed, 64, 1)
            low = low_lanes(packed.shape)
            crosses.append(
                jnp.concatenate(
                    [jnp.where(low, packed, swap), jnp.where(low, swap, packed)], axis=0
                )
            )
        vec, alt = leading_basis(crosses, start_ref[place_ref[0]])
        odd = odd_lanes(vec.shape)
        low = low_lanes(vec.shape)
        upper = jnp.where(odd, -vec, vec).astype(BF16).astype(F32)
        lower = jnp.where(odd, alt, -alt).astype(BF16).astype(F32)
        pivots = total[16 * PAIR : 16 * PAIR + MODES]
        at = jnp.where(low, jnp.stack([pivots, pltpu.roll(pivots, 64, 1)]), 0.0)
        z_re = jnp.sum(upper * at, axis=2, keepdims=True)
        z_im = jnp.sum(lower * at, axis=2, keepdims=True)
        inverse = lax.rsqrt(z_re * z_re + z_im * z_im + 1.0)
        s_re = z_re * inverse
        s_im = z_im * inverse
        expand = jnp.concatenate([upper, lower], axis=1).astype(BF16)
        total = jnp.zeros((MODES, 128), F32) if before is None else rest[1][...]

        lane = lax.broadcasted_iota(jnp.int32, (MODES, 128), 1)
        copies = []
        for half in range(HALVES):
            for fetch in fetches[GROUPS * half : GROUPS * half + GROUPS]:
                fetch.wait()
            span = slice(half * tile, (half + 1) * tile)
            w = w_ref[:, span]
            level_of = deg_ref[:, span]
            base = place_ref[1] + half * bands
            hits = [level_of == base + m for m in range(bands + 1)]
            for f in range(PAIR):
                rows = slice(16 * f, 16 * f + 16)
                x = jnp.concatenate(
                    [held[GROUPS * half + k, rows] for k in range(GROUPS)], axis=0
                )
                psi = jnp.dot(expand[f][:, :64], x, preferred_element_type=F32)
                p_re, p_im = psi[:8], psi[8:]
                out_re = p_re * s_re[f] + p_im * s_im[f]
                out_im = p_im * s_re[f] - p_re * s_im[f]
                stage[half, f, 0] = out_re.astype(BF16)
                stage[half, f, 1] = out_im.astype(BF16)
                power = w * (out_re * out_re + out_im * out_im)
                for m in range(bands + 1):
                    level = jnp.sum(jnp.where(hits[m], power, 0.0), axis=1, keepdims=True)
                    spot = (pair * PAIR + f) * 32 + place_ref[2] + half * bands + m
                    total = total + jnp.where(lane == spot, level * (DEGREES / row_count), 0.0)
            copy = pltpu.make_async_copy(
                stage.at[half],
                modes_ref.at[pl.ds(pair * PAIR, PAIR), :, :, pl.ds(half * tile, tile)],
                sems.at[half],
            )
            copy.start()
            copies.append(copy)
        energy_ref[...] = total
        for copy in copies:
            copy.wait()

    vmem = pl.BlockSpec(memory_space=pltpu.VMEM)
    raw = pl.BlockSpec(memory_space=pl.ANY)
    args = [place, start, weights, degrees, sums, *early, *late]
    source = pl.BlockSpec(memory_space=pltpu.HBM)
    in_specs = [pl.BlockSpec(memory_space=pltpu.SMEM)] + [vmem] * 4 + [source] * (HALVES * GROUPS)
    aliases = {}
    if before is not None:
        in_specs += [raw, vmem]
        aliases = {len(args): 0}
        args += list(before)
    return pl.pallas_call(
        kernel,
        in_specs=in_specs,
        out_specs=[raw, vmem],
        scratch_shapes=[
            pltpu.VMEM((HALVES, PAIR, 2, MODES, tile), BF16),
            pltpu.VMEM((HALVES * GROUPS, 16 * PAIR, tile), BF16),
            pltpu.SemaphoreType.DMA((HALVES,)),
            pltpu.SemaphoreType.DMA((HALVES * GROUPS,)),
        ],
        out_shape=[
            jax.ShapeDtypeStruct((OWNED, 2, MODES, rows_dev), BF16),
            jax.ShapeDtypeStruct((MODES, 128), F32),
        ],
        input_output_aliases=aliases,
        compiler_params=pltpu.CompilerParams(vmem_limit_bytes=SMALL),
        cost_estimate=pl.CostEstimate(
            flops=2 * PAIR * 64 * 256 * rows_dev + 10**9,
            bytes_accessed=PAIR * 2 * 80 * rows_dev,
            transcendentals=0,
        ),
        name="modes",
    )(*args)


def energy_call(gathered):
    chips = gathered.shape[0]

    def kernel(in_ref, out_ref):
        out_ref[...] = jnp.zeros_like(out_ref)
        lane = lax.broadcasted_iota(jnp.int32, (MODES, 128), 1)
        for c in range(chips):
            value = in_ref[c]
            for f in range(OWNED):
                begin = c * 2 * LEVELS
                piece = jnp.where((lane >= 32 * f) & (lane < 32 * f + 2 * LEVELS + 1), value, 0.0)
                shift = (begin - 32 * f) % 128
                piece = pltpu.roll(piece, shift, 1) if shift else piece
                column = begin // 128
                split = 128 - begin % 128
                if split >= 2 * LEVELS + 1:
                    out_ref[f, :, column * 128 : column * 128 + 128] += piece
                else:
                    head = jnp.where(lane >= begin % 128, piece, 0.0)
                    out_ref[f, :, column * 128 : column * 128 + 128] += head
                    if (column + 1) * 128 < DEGREES:
                        out_ref[f, :, (column + 1) * 128 : (column + 2) * 128] += piece - head

    return pl.pallas_call(
        kernel,
        out_shape=jax.ShapeDtypeStruct((OWNED, MODES, DEGREES), F32),
        name="energy",
    )(gathered)


def gather_chips(value):
    value = value + lax.ppermute(value, "core", [(0, 1), (1, 0)])
    chips = STATE[0] * STATE[1]
    spread = jnp.broadcast_to(value[None], (chips,) + value.shape)
    return lax.all_to_all(spread, ("z", "x"), 0, 0, tiled=True)


def after(value, first):
    return lax.optimization_barrier((value, first))[0]


def per_device(snapshots, weights, degrees, pivots):
    rows_dev = snapshots.shape[2]
    row_count = rows_dev * DEVICES
    core = lax.axis_index("core").astype(jnp.int32)
    state = (lax.axis_index(("z", "x", "core"))).astype(jnp.int32)
    y = lax.axis_index("blk").astype(jnp.int32)
    place = jnp.stack([y, state * LEVELS, core * LEVELS])
    pivot_local = (pivots - state * rows_dev)[:, :, None]
    weights = weights.reshape(1, rows_dev)
    degrees = degrees.reshape(1, rows_dev)
    start = jnp.asarray(start_basis())

    halves = [spectra_call(snapshots, half, 4096) for half in range(HALVES)]
    pieces = {}
    for pair in range(PAIR):
        for half in range(HALVES):
            sent = halves[half][pair]
            pieces[pair, half] = [sent[0]] + [
                lax.ppermute(sent[k], "blk", [(g, (g + k) % GROUPS) for g in range(GROUPS)])
                for k in range(1, GROUPS)
            ]
    before = None
    for pair in range(PAIR):
        gram = None
        for half in range(HALVES):
            known = weights if before is None or half < HALVES - 1 else after(weights, before[1])
            gram = gram_call(
                half, pieces[pair, half], known, pivot_local[PAIR * pair : PAIR * pair + PAIR], gram,
                48 if pair == 0 else 40,
            )
        before = modes_call(
            pair, place, start, weights, degrees, gather_chips(gram),
            pieces[pair, 0], pieces[pair, 1], before, row_count,
        )
    modes, energy = before
    return modes, energy_call(gather_chips(energy))


def solution(mesh):
    fine = Mesh(mesh.devices.reshape(*STATE, GROUPS), ("z", "x", "core", "blk"))
    state = ("z", "x", "core")
    return jax.shard_map(
        per_device,
        mesh=fine,
        in_specs=(P("blk", None, state), P(state), P(state), P("blk", None)),
        out_specs=(P("blk", None, None, state), P("blk", None, None)),
        check_vma=False,
    )
```
